256 devices in a mesh: group: 16 (over y, x), local: 16 (over z, core).
Axes of the slice: x: 4, y: 4, z: 8, core: 2. Of those that a mesh axis runs over, the one named last changes fastest.
Arguments:
- event_embed: bfloat16 [1024, 20, 128, 64], P(('group', 'local')), may hold values from -6 to 6
- target: bfloat16 [1024, 20, 64], P(('group', 'local')), may hold values from -6 to 6
- pooled_grad: bfloat16 [1024, 20, 64], P(('group', 'local')), may hold values from -6 to 6
- event_table: int32 [1024, 20, 128], P(('group', 'local')), may hold values from 0 to 127, as said below
- event_row: int32 [1024, 20, 128], P(('group', 'local')), may hold values from 0 to 16383
- table_slot: int32 [128], replicated, may hold values from 0 to 127, as said below
- lengths: int32 [1024, 20], P(('group', 'local')), may hold values from 64 to 128
- caps: int32 [20], replicated, may hold values from 64 to 128, as said below
- w_first: float32 [20, 256, 80], replicated, may hold values from -0.375 to 0.375
- b_first: float32 [20, 80], replicated, may hold values from -3 to 3
- w_second: float32 [20, 80, 40], replicated, may hold values from -0.625 to 0.625
- b_second: float32 [20, 40], replicated, may hold values from -3 to 3
- w_score: float32 [20, 40], replicated, may hold values from -1 to 1
Outputs:
- table_grad: float32 [128, 16384, 64], P('group', 'local')
The draws below stay inside these ranges and needn't reach their ends.
Inputs may be any that keep to these rules, and one draw needn't show every extreme that they name: table_slot is a permutation; the tables with places g * 8 to (g + 1) * 8 - 1 belong to index g of group. `event_table`: the 10240 event slots of one device's samples, padding included, name rows held by any one device (table place // 8 as group index, row // 1024 as local index) at most 60 times, and some device exactly 60 times. `caps`: some feature's cap is 128.
All inputs are finite; a program needn't handle non-finite values.
Results may differ from the reference program's by a relative error of at most 0.0003.
Values sent between devices are 32-bit elements; how exact they have to be, the bound alone decides.
No kernel may reach another device: no remote copies, remote signals or barrier semaphores. Data moves between devices by JAX's collectives and lax.ppermute only.
A program may use at most 128 MiB of HBM per device.

```python
import jax
import jax.numpy as jnp
from jax import lax

D = 64
F = 20
H1 = 80
H2 = 40
LMAX = 128
B_DEV = 4
TAB_OWN = 8
ROWS_DEV = 1024
GROUPS = 16
LOCALS = 16
SAMPLES = 1024
TABLES = 128
ROWS_TAB = 16384
CELL = 40


def shared_places(key):
    return jax.random.permutation(key, TABLES).astype(jnp.int32)


def slot_targets(key):
    dev_count = GROUPS * LOCALS
    slot_count = B_DEV * F * LMAX
    keys = jax.random.split(jax.random.fold_in(key, 11), dev_count)

    def single(sub):
        first_key, second_key, third_key = jax.random.split(sub, 3)
        owners = jax.random.permutation(first_key, dev_count).astype(jnp.int32)
        shares = jax.random.randint(second_key, (dev_count,), 0, CELL // 2 + 1)
        shares = jnp.where(jnp.arange(dev_count) == 1, CELL // 2, shares)
        spots = jnp.arange(slot_count, dtype=jnp.int32)
        cells = spots // CELL
        within = spots % CELL
        moved = (cells % 2 == 1) & (within < shares[cells])
        chosen = owners[jnp.where(moved, cells - 1, cells)]
        mixing = jax.random.permutation(third_key, slot_count)
        return chosen[mixing]
    return jax.vmap(single)(keys)


def draw_table_slot(key, part):
    return shared_places(key)


def draw_event_table(key, part):
    targets = slot_targets(key)
    inverse = jnp.argsort(shared_places(key)).astype(jnp.int32)
    key = jax.random.fold_in(key, 3)
    picks = jax.random.randint(key, targets.shape, 0, TAB_OWN)
    tables = inverse[targets // LOCALS * TAB_OWN + picks]
    return tables.reshape(SAMPLES, F, LMAX).astype(jnp.int32)


def draw_event_row(key, part):
    targets = slot_targets(key)
    key = jax.random.fold_in(key, 4)
    picks = jax.random.randint(key, targets.shape, 0, ROWS_DEV)
    rows = targets % LOCALS * ROWS_DEV + picks
    return rows.reshape(SAMPLES, F, LMAX).astype(jnp.int32)


def draw_caps(key, part):
    key = jax.random.fold_in(key, 5)
    first_key, second_key = jax.random.split(key)
    values = jax.random.randint(first_key, (F,), LMAX // 2, LMAX + 1)
    chosen = jax.random.randint(second_key, (), 0, F)
    return jnp.where(jnp.arange(F) == chosen, LMAX, values).astype(jnp.int32)


def place_ends(values, key, least, largest):
    spot = [jax.random.randint(jax.random.fold_in(key, axis), (), 0, length) for axis, length in enumerate(values.shape)]
    longest = values.shape.index(max(values.shape))
    next_to = spot[:longest] + [(spot[longest] + 1) % values.shape[longest]] + spot[longest + 1:]
    return values.at[tuple(spot)].set(least).at[tuple(next_to)].set(largest)


def steps_of(rng, extent, cuts, low, high):
    level = 1.0
    for axis_at, parts in cuts:
        heights = jax.random.uniform(jax.random.fold_in(jax.random.fold_in(rng, 6), axis_at), (parts,), jnp.float32, low / len(cuts), high / len(cuts))
        level = level * jnp.repeat(jnp.exp(heights), extent[axis_at] // parts).reshape((-1,) + (1,) * (len(extent) - 1 - axis_at))
    return level


def bell_draw(key, extent, scale, bound, cuts=(), kind=jnp.bfloat16):
    entries = scale * jax.random.normal(key, extent, jnp.float32)
    if cuts:
        entries = entries * steps_of(key, extent, cuts, -0.22, 0.18)
    return jnp.clip(entries, -bound, bound).astype(kind)


def setup_inputs(seed: int = 0) -> dict:
    key_list = jax.random.split(jax.random.key(seed), 14)
    event_embed = bell_draw(key_list[0], (SAMPLES, F, LMAX, D), 1.0, 6.0, ((0, 256),))
    target = bell_draw(key_list[1], (SAMPLES, F, D), 1.0, 6.0, ((0, 256),))
    pooled_grad = bell_draw(key_list[2], (SAMPLES, F, D), 1.0, 6.0, ((0, 256),))
    event_table = draw_event_table(jax.random.fold_in(key_list[13], 71), 0)
    event_row = draw_event_row(jax.random.fold_in(key_list[13], 71), 0)
    table_slot = draw_table_slot(jax.random.fold_in(key_list[13], 71), 0)
    lengths = place_ends(jax.random.randint(key_list[6], (SAMPLES, F), LMAX // 2, LMAX + 1), jax.random.fold_in(key_list[6], 1), LMAX // 2, LMAX).astype(jnp.int32)
    caps = draw_caps(jax.random.fold_in(key_list[13], 71), 0)
    w_first = bell_draw(key_list[8], (F, 4 * D, H1), (4 * D) ** -0.5, 0.375, (), jnp.float32)
    b_first = bell_draw(key_list[9], (F, H1), 0.5, 3.0, (), jnp.float32)
    w_second = bell_draw(key_list[10], (F, H1, H2), H1 ** -0.5, 0.625, (), jnp.float32)
    b_second = bell_draw(key_list[11], (F, H2), 0.5, 3.0, (), jnp.float32)
    w_score = bell_draw(key_list[12], (F, H2), H2 ** -0.5, 1.0, (), jnp.float32)
    return {"event_embed": event_embed, "target": target, "pooled_grad": pooled_grad, "event_table": event_table, "event_row": event_row, "table_slot": table_slot, "lengths": lengths, "caps": caps, "w_first": w_first, "b_first": b_first, "w_second": w_second, "b_second": b_second, "w_score": w_score}


def silu_slope(value):
    sig = jax.nn.sigmoid(value)
    return sig * (1.0 + value * (1.0 - sig))


def event_grads(embeds, target, pooled_grad, lengths, caps, w_first, b_first, w_second, b_second, w_score):
    hp = lax.Precision.HIGHEST
    width = embeds.shape[-1]
    vecs = embeds.astype(jnp.float32)
    query = jnp.broadcast_to(target.astype(jnp.float32)[:, :, None, :], vecs.shape)
    joined = jnp.concatenate([vecs, query, vecs * query, vecs - query], axis=-1)
    pre_first = jnp.einsum("nftk,fkh->nfth", joined, w_first, precision=hp) + b_first[None, :, None, :]
    hidden_one = jax.nn.silu(pre_first)
    pre_second = jnp.einsum("nfth,fhj->nftj", hidden_one, w_second, precision=hp) + b_second[None, :, None, :]
    hidden_two = jax.nn.silu(pre_second)
    score = jnp.einsum("nftj,fj->nft", hidden_two, w_score, precision=hp)
    limit = jnp.minimum(lengths, caps[None, :])
    slots = jnp.arange(vecs.shape[2], dtype=jnp.int32)
    kept_mask = (slots[None, None, :] < limit[:, :, None]).astype(jnp.float32)
    upstream = pooled_grad.astype(jnp.float32)[:, :, None, :]
    dscore = jnp.sum(upstream * vecs, axis=-1)
    d_second = dscore[..., None] * w_score[None, :, None, :] * silu_slope(pre_second)
    d_hidden = jnp.einsum("nftj,fhj->nfth", d_second, w_second, precision=hp)
    d_first = d_hidden * silu_slope(pre_first)
    d_joined = jnp.einsum("nfth,fkh->nftk", d_first, w_first, precision=hp)
    total = (score[..., None] * upstream + d_joined[..., :width]
             + d_joined[..., 2 * width:3 * width] * query + d_joined[..., 3 * width:])
    return total * kept_mask[..., None]


def reference(event_embed, target, pooled_grad, event_table, event_row, table_slot, lengths, caps,
              w_first, b_first, w_second, b_second, w_score):
    def single(pieces):
        embeds, query, upstream, length_row = pieces
        return event_grads(embeds[None], query[None], upstream[None], length_row[None], caps,
                           w_first, b_first, w_second, b_second, w_score)[0]

    grads = lax.map(single, (event_embed, target, pooled_grad, lengths))
    places = table_slot[event_table]
    flat_index = (places * ROWS_TAB + event_row).reshape(-1).astype(jnp.int32)
    width = event_embed.shape[-1]
    summed = jnp.zeros((TABLES * ROWS_TAB, width), jnp.float32).at[flat_index].add(grads.reshape(-1, width))
    return summed.reshape(TABLES, ROWS_TAB, width)
```

```python
import functools

import jax
import jax.numpy as jnp
from jax import lax
from jax.experimental import pallas as pl
from jax.experimental.pallas import tpu as pltpu
from jax.sharding import PartitionSpec as P

D = 64
F = 20
H1 = 80
H2 = 40
LMAX = 128
B_DEV = 4
TAB_OWN = 8
ROWS_DEV = 1024
GROUPS = 16
LOCALS = 16
DEVS = GROUPS * LOCALS
PAIRS = B_DEV * F
ROWS_OWN = TAB_OWN * ROWS_DEV
BUCKET = 64
HALF = 32
DUMMY = DEVS * BUCKET
BF = jnp.bfloat16
F32 = jnp.float32
VMEM_BYTES = 56 * 1024 * 1024


def dot(left, right, contract=((1,), (0,))):
    return lax.dot_general(
        left, right, (contract, ((), ())), preferred_element_type=F32
    )


def index_kernel(len_ref, cap_ref, table_ref, row_ref, places_ref, slots_ref, out_ref, dev_ref, own_ref, carry_ref):
    table = table_ref[...]
    place = jnp.take_along_axis(
        jnp.broadcast_to(places_ref[...], table.shape), table, axis=1, mode="promise_in_bounds"
    )
    row = row_ref[...]
    dev_ref[...] = (place >> 3) * LOCALS + (row >> 10)
    own_ref[...] = (place & 7) * ROWS_DEV + (row & 1023)
    carry_ref[...] = jnp.zeros_like(carry_ref)
    out_ref[...] = jnp.zeros_like(out_ref)
    lane = lax.broadcasted_iota(jnp.int32, (1, LMAX), 1)
    dev_iota = lax.broadcasted_iota(jnp.int32, (DEVS, LMAX), 0)
    tri_row = lax.broadcasted_iota(jnp.int32, (LMAX, 2 * LMAX), 0)
    tri_col = lax.broadcasted_iota(jnp.int32, (LMAX, 2 * LMAX), 1)
    earlier = ((tri_row < tri_col)).astype(F32).astype(BF)
    pos_iota = lax.broadcasted_iota(jnp.int32, (2 * BUCKET, LMAX), 0)

    def feature(f, _):
        for n in range(B_DEV):
            p = f * B_DEV + n
            limit = jnp.minimum(len_ref[n, f], cap_ref[f])
            kept = lane < limit
            dev = dev_ref[pl.ds(p, 1), :]
            own = own_ref[pl.ds(p, 1), :]
            hits = dev_iota == jnp.where(kept, dev, -1)
            hot = hits.astype(F32)
            hot_bf = hot.astype(BF)
            counts = dot(hot_bf, earlier)
            before = counts[:, :LMAX] + carry_ref[...]
            carry_ref[...] += counts[:, LMAX:]
            pos = jnp.sum(hot * before, axis=0, keepdims=True).astype(jnp.int32)
            slot = dev * BUCKET + (pos & 1) * HALF + (pos >> 1)
            slots_ref[pl.ds(p, 1), :] = jnp.where(kept, slot, DUMMY)
            value = jnp.where(
                pos_iota < BUCKET, (own >> 7) + 1, own & 127
            )
            spread = jnp.where((pos_iota & (BUCKET - 1)) == pos, value, 0)
            out_ref[...] += dot(hot_bf, spread.astype(F32).astype(BF), ((1,), (1,)))
        return 0

    lax.fori_loop(0, F, feature, 0)
    parts = out_ref[...]
    high = pltpu.roll(parts, BUCKET, 1)
    out_ref[...] = jnp.where(high > 0.0, high * 128.0 + parts - 128.0, float(ROWS_OWN))


def to_column(row, size):
    rows = lax.broadcasted_iota(jnp.int32, (size, row.shape[1]), 0)
    cols = lax.broadcasted_iota(jnp.int32, (size, row.shape[1]), 1)
    return jnp.where(rows == cols, row, 0.0)


def split(value):
    high = value.astype(BF)
    low = (value - high.astype(F32)).astype(BF)
    return high, low


def grad_kernel(
    slots_ref,
    event_ref,
    query_ref,
    up_ref,
    w1_ref,
    b1_ref,
    w2_ref,
    b2_ref,
    ws_ref,
    place_ref,
    out_ref,
    bucket_ref,
    grad_ref,
):
    f = pl.program_id(0)
    w1 = w1_ref[0]
    wa, wb, wc, wd = (w1[:, i * D : (i + 1) * D] for i in range(4))
    wad = wa + wd
    wbd = wb - wd
    wad = jnp.concatenate([wad, wad], axis=1)
    wcc = jnp.concatenate([wc, wc], axis=1)
    zeros = jnp.zeros((H1, D), F32)
    wbd = jnp.concatenate([wbd, zeros], axis=1)
    b1_diag = to_column(
        jnp.concatenate([b1_ref[pl.ds(f, 1), :], jnp.zeros((1, 128 - H1), F32)], axis=1), H1
    )
    b2 = jnp.sum(to_column(b2_ref[pl.ds(f, 1), :], H2), axis=1, keepdims=True)
    ws = jnp.sum(to_column(ws_ref[pl.ds(f, 1), :], H2), axis=1, keepdims=True)
    w2t = w2_ref[0]
    w2t_hi, w2t_lo = split(w2t)
    w2_hi, w2_lo = split(w2t.T)
    w2t_all = jnp.concatenate([w2t_hi, w2t_lo, w2t_hi], axis=1)
    w2_all = jnp.concatenate([w2_hi, w2_lo, w2_hi], axis=1)
    left_half = lax.broadcasted_iota(jnp.int32, (H1, 128), 1) < D
    first_row = lax.broadcasted_iota(jnp.int32, (16, 128), 0) == 0
    row_at = lax.broadcasted_iota(jnp.int32, (16, 128), 0)
    lane_at = lax.broadcasted_iota(jnp.int32, (16, 128), 1)
    for n in range(B_DEV):
        events = event_ref[n, 0]
        query = query_ref[0, n : n + 1, :].astype(F32)
        up = up_ref[0, n : n + 1, :].astype(F32)
        query = jnp.concatenate([query, query], axis=1)
        up = jnp.concatenate([up, up], axis=1)
        folded = wad + wcc * query
        fold_hi = folded.astype(BF)
        fold_rest = folded - fold_hi.astype(F32)
        fold_lo = fold_rest.astype(BF)
        offset = jnp.sum(wbd * query + b1_diag, axis=1, keepdims=True)
        both = jnp.where(left_half, fold_hi.astype(F32), fold_rest).astype(BF)
        up_row = jnp.where((row_at == 0) & (lane_at < D), up, 0.0).astype(BF)
        first = dot(
            jnp.concatenate([both, up_row], axis=0), jnp.concatenate([events, events], axis=0)
        )
        pre1 = first[:H1] + offset
        dscore = first[H1 : H1 + 1]
        sig1 = 0.5 + 0.5 * jnp.tanh(0.5 * pre1)
        h1 = pre1 * sig1
        slope1 = sig1 + h1 * (1.0 - sig1)
        h1_hi, h1_lo = split(h1)
        pre2 = dot(w2t_all, jnp.concatenate([h1_hi, h1_hi, h1_lo], axis=0)) + b2
        sig2 = 0.5 + 0.5 * jnp.tanh(0.5 * pre2)
        h2 = pre2 * sig2
        slope2 = sig2 + h2 * (1.0 - sig2)
        score = jnp.sum(h2 * ws, axis=0, keepdims=True)
        d2 = (dscore * ws) * slope2
        d2_hi, d2_lo = split(d2)
        d1 = dot(w2_all, jnp.concatenate([d2_hi, d2_hi, d2_lo], axis=0)) * slope1
        d1_hi, d1_lo = split(d1)
        score_hi = score.astype(BF).astype(F32)
        score_rows = jnp.where(
            row_at == 0, score_hi, jnp.where(row_at == 1, score - score_hi, 0.0)
        ).astype(BF)
        up_rows = jnp.where(row_at < 2, up, 0.0).astype(BF)
        grad_ref[n * LMAX : (n + 1) * LMAX, :] = dot(
            jnp.concatenate([d1_hi, d1_lo, d1_hi, score_rows], axis=0),
            jnp.concatenate([fold_hi, fold_hi, fold_lo, up_rows], axis=0),
            ((0,), (0,)),
        )
    base = f * (B_DEV * LMAX)

    for t in range(B_DEV * LMAX):
        slot = slots_ref[base + t]
        bucket_ref[pl.ds(slot, 1), :] = grad_ref[t : t + 1, :]

    @pl.when(f == F - 1)
    def _():
        lanes = lax.broadcasted_iota(jnp.int32, (HALF, 128), 1) < D

        def pack(dev, _):
            at = pl.multiple_of(dev * BUCKET, BUCKET)
            bucket_ref[pl.ds(at + BUCKET - 1, 1), :] = place_ref[pl.ds(dev, 1), :]
            left = bucket_ref[pl.ds(at, HALF), :]
            right = bucket_ref[pl.ds(pl.multiple_of(at + HALF, HALF), HALF), :]
            out_ref[dev] = jnp.where(lanes, left, right)
            return 0

        lax.fori_loop(0, DEVS, pack, 0, unroll=4)


def landing_kernel(tail_ref, out_ref):
    values = tail_ref[:, 7, :].astype(jnp.int32)
    lane = lax.broadcasted_iota(jnp.int32, values.shape, 1)
    filled = (lane >= D) & (values < ROWS_OWN)
    count = jnp.sum(filled.astype(jnp.int32), axis=1, keepdims=True)
    clash = jnp.zeros(values.shape, jnp.int32)
    for shift in range(2, 16, 2):
        moved = pltpu.roll(values, shift, 1)
        same = filled & (moved == values) & ((lane & 15) >= shift)
        clash = clash | same.astype(jnp.int32)
    clashes = jnp.sum(clash, axis=1, keepdims=True)
    batches = (count + 15) >> 4
    result = jnp.where(lane == 0, batches, values)
    out_ref[...] = jnp.where(lane == 1, clashes, result)


def add_kernel(land_ref, in_ref, out_ref, left_ref, right_ref):
    def clear(i, _):
        at = pl.multiple_of(i * 64, 64)
        left_ref[pl.ds(at, 64), :] = jnp.zeros((64, 128), F32)
        right_ref[pl.ds(at, 64), :] = jnp.zeros((64, 128), F32)
        return 0

    lax.fori_loop(0, ROWS_OWN // 64, clear, 0)

    def source(s, _):
        base = s * 128
        batches = land_ref[base]
        clashes = land_ref[base + 1]

        def batch(b, _):
            at = base + D + b * 16
            row = s * HALF + b * 8
            spots_l = [land_ref[at + 2 * j] for j in range(8)]
            spots_r = [land_ref[at + 2 * j + 1] for j in range(8)]
            news = [in_ref[pl.ds(row + j, 1), :] for j in range(8)]
            left = [left_ref[pl.ds(spots_l[j], 1), :] + news[j] for j in range(8)]
            right = [right_ref[pl.ds(spots_r[j], 1), :] + news[j] for j in range(8)]
            for j in range(8):
                left_ref[pl.ds(spots_l[j], 1), :] = left[j]
            for j in range(8):
                right_ref[pl.ds(spots_r[j], 1), :] = right[j]
            return 0

        def single(j, _):
            at = base + D + 2 * j
            spot_l = land_ref[at]
            spot_r = land_ref[at + 1]
            new = in_ref[pl.ds(s * HALF + j, 1), :]
            left_ref[pl.ds(spot_l, 1), :] += new
            right_ref[pl.ds(spot_r, 1), :] += new
            return 0

        @pl.when(clashes == 0)
        def _():
            lax.fori_loop(0, batches, batch, 0)

        @pl.when(clashes != 0)
        def _():
            lax.fori_loop(0, batches * 8, single, 0)

        return 0

    lax.fori_loop(0, DEVS, source, 0)
    lanes = lax.broadcasted_iota(jnp.int32, (128, 128), 1) < D

    for table in range(TAB_OWN):
        for block in range(ROWS_DEV // 128):
            at = table * ROWS_DEV + block * 128
            joined = jnp.where(lanes, left_ref[at : at + 128, :], right_ref[at : at + 128, :])
            turned = joined.T
            out_ref[table, :, block * 128 : (block + 1) * 128] = turned[:D] + turned[D:]


def params(semantics=None):
    return pltpu.CompilerParams(vmem_limit_bytes=VMEM_BYTES, dimension_semantics=semantics)


def find_slots(lengths, caps, table, row, places):
    smem = pl.BlockSpec(memory_space=pltpu.SMEM)
    vmem = pl.BlockSpec(memory_space=pltpu.VMEM)
    return pl.pallas_call(
        index_kernel,
        in_specs=[smem, smem, vmem, vmem, vmem],
        out_specs=[vmem, vmem],
        out_shape=[
            jax.ShapeDtypeStruct((PAIRS, LMAX), jnp.int32),
            jax.ShapeDtypeStruct((DEVS, LMAX), F32),
        ],
        scratch_shapes=[
            pltpu.VMEM((PAIRS, LMAX), jnp.int32),
            pltpu.VMEM((PAIRS, LMAX), jnp.int32),
            pltpu.VMEM((DEVS, LMAX), F32),
        ],
        compiler_params=params(),
    )(lengths, caps, table, row, places)


def pack_grads(slots, events, query, up, w1, b1, w2, b2, ws, place):
    whole = lambda shape: pl.BlockSpec(shape, lambda f, s: (0,) * len(shape))
    return pl.pallas_call(
        grad_kernel,
        grid_spec=pltpu.PrefetchScalarGridSpec(
            num_scalar_prefetch=1,
            grid=(F,),
            in_specs=[
                pl.BlockSpec((B_DEV, 1, D, LMAX), lambda f, s: (0, f, 0, 0)),
                pl.BlockSpec((1, B_DEV, D), lambda f, s: (f, 0, 0)),
                pl.BlockSpec((1, B_DEV, D), lambda f, s: (f, 0, 0)),
                pl.BlockSpec((1, H1, 4 * D), lambda f, s: (f, 0, 0)),
                whole((F, H1)),
                pl.BlockSpec((1, H2, H1), lambda f, s: (f, 0, 0)),
                whole((F, H2)),
                whole((F, H2)),
                whole((DEVS, LMAX)),
            ],
            out_specs=pl.BlockSpec((DEVS, HALF, 128), lambda f, s: (0, 0, 0)),
            scratch_shapes=[
                pltpu.VMEM((DUMMY + 8, 128), F32),
                pltpu.VMEM((B_DEV * LMAX, 128), F32),
            ],
        ),
        out_shape=jax.ShapeDtypeStruct((DEVS, HALF, 128), F32),
        compiler_params=params(("arbitrary",)),
    )(slots, events, query, up, w1, b1, w2, b2, ws, place)


def find_landing(arrived):
    return pl.pallas_call(
        landing_kernel,
        grid=(1,),
        in_specs=[pl.BlockSpec((DEVS, 8, 128), lambda i: (0, 3, 0))],
        out_specs=pl.BlockSpec((DEVS, 128), lambda i: (0, 0)),
        out_shape=jax.ShapeDtypeStruct((DEVS, 128), jnp.int32),
        compiler_params=params(("arbitrary",)),
    )(arrived)


def add_rows(landing, arrived):
    return pl.pallas_call(
        add_kernel,
        grid_spec=pltpu.PrefetchScalarGridSpec(
            num_scalar_prefetch=1,
            grid=(1,),
            in_specs=[pl.BlockSpec((DEVS * HALF, 128), lambda i, s: (0, 0))],
            out_specs=pl.BlockSpec((TAB_OWN, D, ROWS_DEV), lambda i, s: (0, 0, 0)),
            scratch_shapes=[
                pltpu.VMEM((ROWS_OWN + 8, 128), F32),
                pltpu.VMEM((ROWS_OWN + 8, 128), F32),
            ],
        ),
        out_shape=jax.ShapeDtypeStruct((TAB_OWN, D, ROWS_DEV), F32),
        compiler_params=params(("arbitrary",)),
    )(landing, arrived)


def send_side(
    event_embed, target, pooled_grad, event_table, event_row, table_slot, lengths, caps,
    w_first, b_first, w_second, b_second, w_score,
):
    table = event_table.transpose(1, 0, 2).reshape(PAIRS, LMAX)
    row = event_row.transpose(1, 0, 2).reshape(PAIRS, LMAX)
    slots, place = find_slots(lengths, caps, table, row, table_slot.reshape(1, -1))
    return pack_grads(
        slots.reshape(-1),
        event_embed.transpose(0, 1, 3, 2),
        target.transpose(1, 0, 2),
        pooled_grad.transpose(1, 0, 2),
        w_first.transpose(0, 2, 1),
        b_first,
        w_second.transpose(0, 2, 1),
        b_second,
        w_score,
        place,
    )


def receive_side(arrived):
    landing = find_landing(arrived)
    summed = add_rows(landing.reshape(-1), arrived.reshape(DEVS * HALF, 128))
    return summed.transpose(0, 2, 1)


def per_device(*args):
    packed = send_side(*args)
    arrived = lax.all_to_all(packed, ("group", "local"), split_axis=0, concat_axis=0, tiled=True)
    return receive_side(arrived)


def solution(mesh):
    split_all = ("group", "local")
    in_specs = (
        P(split_all, None, None, None),
        P(split_all, None, None),
        P(split_all, None, None),
        P(split_all, None, None),
        P(split_all, None, None),
        P(),
        P(split_all, None),
        P(),
        P(),
        P(),
        P(),
        P(),
        P(),
    )
    return jax.shard_map(
        per_device, mesh=mesh, in_specs=in_specs, out_specs=P("group", "local", None), check_vma=False
    )
```

```python
import functools

import jax
import jax.numpy as jnp
from jax import lax
from jax.experimental import pallas as pl
from jax.experimental.pallas import tpu as pltpu
from jax.sharding import PartitionSpec as P

D = 64
F = 20
H1 = 80
H2 = 40
H2_PAD = 48
STEP = 2
RANK_STEP = 4
ADD_STEP = 4
CHUNK = 32
LMAX = 128
B_DEV = 4
TAB_OWN = 8
ROWS_DEV = 1024
GROUPS = 16
LOCALS = 16
DEVS = GROUPS * LOCALS
PAIRS = B_DEV * F
ROWS_OWN = TAB_OWN * ROWS_DEV
BUCKET = 64
HALF = 32
DUMMY = DEVS * BUCKET
BF = jnp.bfloat16
F32 = jnp.float32
VMEM_BYTES = 56 * 1024 * 1024


def dot(left, right, contract=((1,), (0,))):
    return lax.dot_general(
        left, right, (contract, ((), ())), preferred_element_type=F32
    )


def index_kernel(len_ref, cap_ref, table_ref, row_ref, places_ref, slots_ref, out_ref, dev_ref, own_ref, carry_ref):
    table = table_ref[...]
    place = jnp.take_along_axis(
        jnp.broadcast_to(places_ref[...], table.shape), table, axis=1, mode="promise_in_bounds"
    )
    row = row_ref[...]
    dev_ref[...] = (place >> 3) * LOCALS + (row >> 10)
    own_ref[...] = (place & 7) * ROWS_DEV + (row & 1023)
    carry_ref[...] = jnp.zeros_like(carry_ref)
    out_ref[...] = jnp.zeros_like(out_ref)
    span = B_DEV * LMAX
    lane = lax.broadcasted_iota(jnp.int32, (1, LMAX), 1)
    dev_iota = lax.broadcasted_iota(jnp.int32, (DEVS, LMAX), 0)
    tri_row = lax.broadcasted_iota(jnp.int32, (span, span + LMAX), 0)
    tri_col = lax.broadcasted_iota(jnp.int32, (span, span + LMAX), 1)
    earlier = (tri_row < tri_col).astype(F32).astype(BF)
    pos_iota = lax.broadcasted_iota(jnp.int32, (BUCKET, LMAX), 0)

    def features(i, _):
        hits, counts, hots, owns, keeps, devs = [], [], [], [], [], []
        for k in range(RANK_STEP):
            f = i * RANK_STEP + k
            for n in range(B_DEV):
                p = f * B_DEV + n
                kept = lane < jnp.minimum(len_ref[n, f], cap_ref[f])
                dev = dev_ref[pl.ds(p, 1), :]
                keeps.append(kept)
                devs.append(dev)
                owns.append(own_ref[pl.ds(p, 1), :])
                hits.append(dev_iota == jnp.where(kept, dev, -1))
            hot = jnp.concatenate(
                [jnp.where(hits[k * B_DEV + n], 1.0, 0.0).astype(BF) for n in range(B_DEV)], axis=1
            )
            hots.append(hot)
            counts.append(dot(hot, earlier))
        carry = carry_ref[...]
        total = out_ref[...]
        for k in range(RANK_STEP):
            spreads = []
            for n in range(B_DEV):
                at = k * B_DEV + n
                before = counts[k][:, n * LMAX : (n + 1) * LMAX] + carry
                pos = jnp.sum(jnp.where(hits[at], before, 0.0), axis=0, keepdims=True)
                pos = pos.astype(jnp.int32)
                slot = devs[at] * BUCKET + (pos & 1) * HALF + (pos >> 1)
                slots_ref[pl.ds(i * (RANK_STEP * B_DEV) + at, 1), :] = jnp.where(
                    keeps[at], slot, DUMMY
                )
                high = ((owns[at] >> 7) + 1).astype(F32)
                low = (owns[at] & 127).astype(F32)
                same = pos_iota == pos
                spreads.append(
                    jnp.concatenate(
                        [jnp.where(same, high, 0.0).astype(BF), jnp.where(same, low, 0.0).astype(BF)],
                        axis=0,
                    )
                )
            total = total + dot(hots[k], jnp.concatenate(spreads, axis=1), ((1,), (1,)))
            carry = carry + counts[k][:, span:]
        carry_ref[...] = carry
        out_ref[...] = total
        return 0

    lax.fori_loop(0, F // RANK_STEP, features, 0)
    parts = out_ref[...]
    high = pltpu.roll(parts, BUCKET, 1)
    out_ref[...] = jnp.where(high > 0.0, high * 128.0 + parts - 128.0, float(ROWS_OWN))


def to_column(row, size):
    rows = lax.broadcasted_iota(jnp.int32, (size, row.shape[1]), 0)
    cols = lax.broadcasted_iota(jnp.int32, (size, row.shape[1]), 1)
    return jnp.where(rows == cols, row, 0.0)


def split(value):
    high = value.astype(BF)
    low = (value - high.astype(F32)).astype(BF)
    return high, low


def grad_kernel(
    slots_ref,
    event_ref,
    query_ref,
    up_ref,
    w1_ref,
    b1_ref,
    w2_ref,
    b2_ref,
    ws_ref,
    place_ref,
    out_ref,
    bucket_ref,
    grad_ref,
    pack_ref,
    sems,
):
    step = pl.program_id(0)

    def scatter(base):
        for t in range(STEP * B_DEV * LMAX):
            slot = slots_ref[base + t]
            bucket_ref[pl.ds(slot, 1), :] = grad_ref[t : t + 1, :]

    scatter(jnp.maximum(step - 1, 0) * (STEP * B_DEV * LMAX))
    left_half = lax.broadcasted_iota(jnp.int32, (H1, 128), 1) < D
    row_at = lax.broadcasted_iota(jnp.int32, (16, 128), 0)
    lane_at = lax.broadcasted_iota(jnp.int32, (16, 128), 1)
    folds, ups, pre1, dscore, b2, ws, w2t_all, w2_all = ([] for _ in range(8))
    for k in range(STEP):
        f = step * STEP + k
        w1 = w1_ref[k]
        wa, wb, wc, wd = (w1[:, i * D : (i + 1) * D] for i in range(4))
        wad = wa + wd
        wbd = wb - wd
        wad = jnp.concatenate([wad, wad], axis=1)
        wcc = jnp.concatenate([wc, wc], axis=1)
        wbd = jnp.concatenate([wbd, jnp.zeros((H1, D), F32)], axis=1)
        b1_diag = to_column(
            jnp.concatenate([b1_ref[pl.ds(f, 1), :], jnp.zeros((1, 128 - H1), F32)], axis=1), H1
        )
        b2.append(jnp.sum(to_column(b2_ref[pl.ds(f, 1), :], H2_PAD), axis=1, keepdims=True))
        ws.append(jnp.sum(to_column(ws_ref[pl.ds(f, 1), :], H2_PAD), axis=1, keepdims=True))
        w2t = jnp.concatenate([w2_ref[k], jnp.zeros((H2_PAD - H2, H1), F32)], axis=0)
        w2t_hi, w2t_lo = split(w2t)
        w2_hi, w2_lo = split(w2t.T)
        w2t_all.append(jnp.concatenate([w2t_hi, w2t_lo, w2t_hi], axis=1))
        w2_all.append(jnp.concatenate([w2_hi, w2_lo, w2_hi], axis=1))
        firsts = []
        for n in range(B_DEV):
            events = event_ref[n, k]
            query = query_ref[k, n : n + 1, :].astype(F32)
            up = up_ref[k, n : n + 1, :].astype(F32)
            query = jnp.concatenate([query, query], axis=1)
            up = jnp.concatenate([up, up], axis=1)
            folded = wad + wcc * query
            fold_hi = folded.astype(BF)
            fold_rest = folded - fold_hi.astype(F32)
            offset = jnp.sum(wbd * query + b1_diag, axis=1, keepdims=True)
            both = jnp.where(left_half, fold_hi.astype(F32), fold_rest).astype(BF)
            up_row = jnp.where((row_at == 0) & (lane_at < D), up, 0.0).astype(BF)
            first = dot(
                jnp.concatenate([both, up_row], axis=0), jnp.concatenate([events, events], axis=0)
            )
            firsts.append((first[:H1] + offset, first[H1 : H1 + 1]))
            folds.append((fold_hi, fold_rest.astype(BF)))
            ups.append(jnp.where(row_at < 2, up, 0.0).astype(BF))
        pre1.append(jnp.concatenate([first[0] for first in firsts], axis=1))
        dscore.append(jnp.concatenate([first[1] for first in firsts], axis=1))
    pre2, slope1, score, d1 = [], [], [], []
    for k in range(STEP):
        sig1 = 0.5 + 0.5 * jnp.tanh(0.5 * pre1[k])
        h1 = pre1[k] * sig1
        slope1.append(sig1 + h1 * (1.0 - sig1))
        h1_hi, h1_lo = split(h1)
        pre2.append(dot(w2t_all[k], jnp.concatenate([h1_hi, h1_hi, h1_lo], axis=0)) + b2[k])
    for k in range(STEP):
        sig2 = 0.5 + 0.5 * jnp.tanh(0.5 * pre2[k])
        h2 = pre2[k] * sig2
        slope2 = sig2 + h2 * (1.0 - sig2)
        score.append(jnp.sum(h2 * ws[k], axis=0, keepdims=True))
        d2_hi, d2_lo = split((dscore[k] * ws[k]) * slope2)
        d1.append(dot(w2_all[k], jnp.concatenate([d2_hi, d2_hi, d2_lo], axis=0)))
    for k in range(STEP):
        d1_hi, d1_lo = split(d1[k] * slope1[k])
        score_hi = score[k].astype(BF).astype(F32)
        score_lo = score[k] - score_hi
        for n in range(B_DEV):
            at = slice(n * LMAX, (n + 1) * LMAX)
            score_rows = jnp.where(
                row_at == 0, score_hi[:, at], jnp.where(row_at == 1, score_lo[:, at], 0.0)
            ).astype(BF)
            fold_hi, fold_lo = folds[k * B_DEV + n]
            row = (k * B_DEV + n) * LMAX
            grad_ref[row : row + LMAX, :] = dot(
                jnp.concatenate([d1_hi[:, at], d1_lo[:, at], d1_hi[:, at], score_rows], axis=0),
                jnp.concatenate([fold_hi, fold_hi, fold_lo, ups[k * B_DEV + n]], axis=0),
                ((0,), (0,)),
            )

    @pl.when(step == F // STEP - 1)
    def _():
        scatter(step * (STEP * B_DEV * LMAX))
        lanes = lax.broadcasted_iota(jnp.int32, (HALF, 128), 1) < D

        def pack(chunk, _):
            def one(k, _):
                dev = chunk * CHUNK + k
                at = pl.multiple_of(dev * BUCKET, BUCKET)
                bucket_ref[pl.ds(at + BUCKET - 1, 1), :] = place_ref[pl.ds(dev, 1), :]
                left = bucket_ref[pl.ds(at, HALF), :]
                right = bucket_ref[pl.ds(pl.multiple_of(at + HALF, HALF), HALF), :]
                pack_ref[dev] = jnp.where(lanes, left, right)
                return 0

            lax.fori_loop(0, CHUNK, one, 0, unroll=8)
            part = pl.ds(chunk * CHUNK, CHUNK)
            pltpu.make_async_copy(pack_ref.at[part], out_ref.at[part], sems.at[chunk]).start()
            return 0

        def finish(chunk, _):
            part = pl.ds(chunk * CHUNK, CHUNK)
            pltpu.make_async_copy(pack_ref.at[part], out_ref.at[part], sems.at[chunk]).wait()
            return 0

        lax.fori_loop(0, DEVS // CHUNK, pack, 0)
        lax.fori_loop(0, DEVS // CHUNK, finish, 0)


def add_kernel(in_ref, out_ref, new_ref, tail_ref, spot_ref, land_ref, turn_ref, sems, *sums):
    whole = pltpu.make_async_copy(in_ref, new_ref, sems.at[0])
    tails = pltpu.make_async_copy(in_ref.at[:, HALF - 8 :, :], tail_ref, sems.at[1])
    tails.start()
    whole.start()

    def clear(i, _):
        at = pl.multiple_of(i * 64, 64)
        for total in sums:
            total[pl.ds(at, 64), :] = jnp.zeros((64, 128), F32)
        return 0

    lax.fori_loop(0, ROWS_OWN // 64, clear, 0)
    tails.wait()
    values = tail_ref[:, 7, :].astype(jnp.int32)
    lane = lax.broadcasted_iota(jnp.int32, values.shape, 1)
    filled = (lane >= D) & (values < ROWS_OWN)
    count = jnp.sum(filled.astype(jnp.int32), axis=1, keepdims=True)
    clash = jnp.zeros(values.shape, jnp.int32)
    for shift in range(2, 16, 2):
        moved = pltpu.roll(values, shift, 1)
        same = filled & (moved == values) & ((lane & 15) >= shift)
        clash = clash | same.astype(jnp.int32)
    clashes = jnp.sum(clash, axis=1, keepdims=True)
    later = pltpu.roll(jnp.where(clash > 0, values, ROWS_OWN), D, 1)
    spots = jnp.where(lane < D, later, jnp.where(clash > 0, ROWS_OWN, values))
    mode = jnp.where(count > 32, 1, 0) + jnp.where(clashes > 0, 2, 0)
    spots = jnp.where(lane == 60, mode, jnp.where(lane == 61, count, spots))
    spot_ref[...] = spots
    spots = pltpu.make_async_copy(spot_ref, land_ref, sems.at[2])
    spots.start()
    spots.wait()
    whole.wait()

    def batch(s, start):
        parts = []
        for b in range(2):
            row = start + b * 8
            for side in range(2):
                total = sums[2 * b + side]
                at = [land_ref[s, D + 2 * (row + j) + side] for j in range(8)]
                add = [
                    total[pl.ds(at[j], 1), :] + new_ref[s, pl.ds(row + j, 1), :] for j in range(8)
                ]
                parts.append((total, at, add))
        for total, at, add in parts:
            for j in range(8):
                total[pl.ds(at[j], 1), :] = add[j]

    def sources(i, _):
        for k in range(ADD_STEP):
            batch(i * ADD_STEP + k, 0)
        for k in range(ADD_STEP):
            s = i * ADD_STEP + k
            mode = land_ref[s, 60]

            @pl.when(mode > 0)
            def _():
                @pl.when((mode & 1) == 1)
                def _():
                    batch(s, 16)

                @pl.when(mode >= 2)
                def _():
                    def single(j, _):
                        new = new_ref[s, pl.ds(j, 1), :]
                        for side in range(2):
                            sums[side][pl.ds(land_ref[s, 2 * j + side], 1), :] += new
                        return 0

                    lax.fori_loop(0, (land_ref[s, 61] + 1) >> 1, single, 0)

        return 0

    lax.fori_loop(0, DEVS // ADD_STEP, sources, 0)
    lanes = lax.broadcasted_iota(jnp.int32, (128, 128), 1) < D
    for table in range(TAB_OWN):
        for block in range(ROWS_DEV // 128):
            at = table * ROWS_DEV + block * 128
            at = slice(at, at + 128)
            joined = jnp.where(
                lanes, sums[0][at, :] + sums[2][at, :], sums[1][at, :] + sums[3][at, :]
            )
            turned = joined.T
            turn_ref[table, :, block * 128 : (block + 1) * 128] = turned[:D] + turned[D:]
        pltpu.make_async_copy(turn_ref.at[table], out_ref.at[table], sems.at[3 + table]).start()
    for table in range(TAB_OWN):
        pltpu.make_async_copy(turn_ref.at[table], out_ref.at[table], sems.at[3 + table]).wait()


def params(semantics=None):
    return pltpu.CompilerParams(vmem_limit_bytes=VMEM_BYTES, dimension_semantics=semantics)


def find_slots(lengths, caps, table, row, places):
    smem = pl.BlockSpec(memory_space=pltpu.SMEM)
    vmem = pl.BlockSpec(memory_space=pltpu.VMEM)
    return pl.pallas_call(
        index_kernel,
        in_specs=[smem, smem, vmem, vmem, vmem],
        out_specs=[vmem, vmem],
        out_shape=[
            jax.ShapeDtypeStruct((PAIRS, LMAX), jnp.int32),
            jax.ShapeDtypeStruct((DEVS, LMAX), F32),
        ],
        scratch_shapes=[
            pltpu.VMEM((PAIRS, LMAX), jnp.int32),
            pltpu.VMEM((PAIRS, LMAX), jnp.int32),
            pltpu.VMEM((DEVS, LMAX), F32),
        ],
        compiler_params=params(),
    )(lengths, caps, table, row, places)


def pack_grads(slots, events, query, up, w1, b1, w2, b2, ws, place):
    whole = lambda shape: pl.BlockSpec(shape, lambda f, s: (0,) * len(shape))
    return pl.pallas_call(
        grad_kernel,
        grid_spec=pltpu.PrefetchScalarGridSpec(
            num_scalar_prefetch=1,
            grid=(F // STEP,),
            in_specs=[
                pl.BlockSpec((B_DEV, STEP, D, LMAX), lambda f, s: (0, f, 0, 0)),
                pl.BlockSpec((STEP, B_DEV, D), lambda f, s: (f, 0, 0)),
                pl.BlockSpec((STEP, B_DEV, D), lambda f, s: (f, 0, 0)),
                pl.BlockSpec((STEP, H1, 4 * D), lambda f, s: (f, 0, 0)),
                whole((F, H1)),
                pl.BlockSpec((STEP, H2, H1), lambda f, s: (f, 0, 0)),
                whole((F, H2)),
                whole((F, H2)),
                whole((DEVS, LMAX)),
            ],
            out_specs=pl.BlockSpec(memory_space=pl.ANY),
            scratch_shapes=[
                pltpu.VMEM((DUMMY + 8, 128), F32),
                pltpu.VMEM((STEP * B_DEV * LMAX, 128), F32),
                pltpu.VMEM((DEVS, HALF, 128), F32),
                pltpu.SemaphoreType.DMA((DEVS // CHUNK,)),
            ],
        ),
        out_shape=jax.ShapeDtypeStruct((DEVS, HALF, 128), F32),
        compiler_params=params(("arbitrary",)),
    )(slots, events, query, up, w1, b1, w2, b2, ws, place)


def add_rows(arrived):
    return pl.pallas_call(
        add_kernel,
        in_specs=[pl.BlockSpec(memory_space=pl.ANY)],
        out_specs=pl.BlockSpec(memory_space=pl.ANY),
        out_shape=jax.ShapeDtypeStruct((TAB_OWN, D, ROWS_DEV), F32),
        scratch_shapes=[
            pltpu.VMEM((DEVS, HALF, 128), F32),
            pltpu.VMEM((DEVS, 8, 128), F32),
            pltpu.VMEM((DEVS, 128), jnp.int32),
            pltpu.SMEM((DEVS, 128), jnp.int32),
            pltpu.VMEM((TAB_OWN, D, ROWS_DEV), F32),
            pltpu.SemaphoreType.DMA((3 + TAB_OWN,)),
        ]
        + [pltpu.VMEM((ROWS_OWN + 8, 128), F32)] * 4,
        compiler_params=params(),
    )(arrived)


def send_side(
    event_embed, target, pooled_grad, event_table, event_row, table_slot, lengths, caps,
    w_first, b_first, w_second, b_second, w_score,
):
    table = event_table.transpose(1, 0, 2).reshape(PAIRS, LMAX)
    row = event_row.transpose(1, 0, 2).reshape(PAIRS, LMAX)
    slots, place = find_slots(lengths, caps, table, row, table_slot.reshape(1, -1))
    return pack_grads(
        slots.reshape(-1),
        event_embed.transpose(0, 1, 3, 2),
        target.transpose(1, 0, 2),
        pooled_grad.transpose(1, 0, 2),
        w_first.transpose(0, 2, 1),
        b_first,
        w_second.transpose(0, 2, 1),
        b_second,
        w_score,
        place,
    )


def receive_side(arrived):
    return add_rows(arrived).transpose(0, 2, 1)


def per_device(*args):
    packed = send_side(*args)
    arrived = lax.all_to_all(packed, ("group", "local"), split_axis=0, concat_axis=0, tiled=True)
    return receive_side(arrived)


def solution(mesh):
    split_all = ("group", "local")
    in_specs = (
        P(split_all, None, None, None),
        P(split_all, None, None),
        P(split_all, None, None),
        P(split_all, None, None),
        P(split_all, None, None),
        P(),
        P(split_all, None),
        P(),
        P(),
        P(),
        P(),
        P(),
        P(),
    )
    return jax.shard_map(
        per_device, mesh=mesh, in_specs=in_specs, out_specs=P("group", "local", None), check_vma=False
    )
```

```python
import functools

import jax
import jax.numpy as jnp
from jax import lax
from jax.experimental import pallas as pl
from jax.experimental.pallas import tpu as pltpu
from jax.sharding import PartitionSpec as P

D = 64
F = 20
H1 = 80
H2 = 40
H2_PAD = 48
LMAX = 128
B_DEV = 4
TAB_OWN = 8
ROWS_DEV = 1024
LOCALS = 16
DEVS = 256
PAIRS = B_DEV * F
ROWS_OWN = TAB_OWN * ROWS_DEV
STEP = 2
STEPS = F // STEP
SPAN = STEP * B_DEV
EVENTS = SPAN * LMAX
BLOCK = 2 * LMAX
BUCKET = 64
HALF = 32
ROWS = 28
MAIN = 2 * ROWS - 1
LATE = HALF - ROWS
PLACES = 60
DUMMY = DEVS * BUCKET
CHUNK = 32
PIECES = 4
PIECE = DEVS // PIECES
ADD_STEP = 4
BF = jnp.bfloat16
F32 = jnp.float32
VMEM_BYTES = 63 * 1024 * 1024


def dot(left, right, contract=((1,), (0,))):
    return lax.dot_general(left, right, (contract, ((), ())), preferred_element_type=F32)


def diagonal(row, size):
    rows = lax.broadcasted_iota(jnp.int32, (size, row.shape[1]), 0)
    cols = lax.broadcasted_iota(jnp.int32, (size, row.shape[1]), 1)
    return jnp.where(rows == cols, row, 0.0)


def split(value):
    high = value.astype(BF)
    low = (value - high.astype(F32)).astype(BF)
    return high, low


def rank_events(step, len_ref, cap_ref, table_ref, row_ref, places_ref, earlier_ref, carry_ref, place_ref, slots_ref):
    table = table_ref[...]
    place = jnp.take_along_axis(
        jnp.broadcast_to(places_ref[...], table.shape), table, axis=1, mode="promise_in_bounds"
    )
    row = row_ref[...]
    devs = (place >> 3) * LOCALS + (row >> 10)
    owns = (place & 7) * ROWS_DEV + (row & 1023)
    highs = ((owns >> 7) + 1).astype(F32)
    lows = (owns & 127).astype(F32)
    lane = lax.broadcasted_iota(jnp.int32, (1, LMAX), 1)
    dev_iota = lax.broadcasted_iota(jnp.int32, (DEVS, LMAX), 0)
    pos_iota = lax.broadcasted_iota(jnp.int32, (BUCKET, LMAX), 0)
    keeps, hits, hots, counts = [], [], [], []
    for p in range(SPAN):
        f = step * STEP + p // B_DEV
        kept = lane < jnp.minimum(len_ref[p % B_DEV, f], cap_ref[f])
        keeps.append(kept)
        hits.append(dev_iota == jnp.where(kept, devs[p : p + 1], -1))
    for p in range(0, SPAN, 2):
        hot = jnp.concatenate(
            [jnp.where(hits[p + k], 1.0, 0.0).astype(BF) for k in range(2)], axis=1
        )
        hots.append(hot)
        counts.append(dot(hot, earlier_ref[...]))
    carry = carry_ref[...]
    total = place_ref[...]
    for b in range(SPAN // 2):
        spreads = []
        for k in range(2):
            p = 2 * b + k
            before = counts[b][:, k * LMAX : (k + 1) * LMAX] + carry
            pos = jnp.sum(jnp.where(hits[p], before, 0.0), axis=0, keepdims=True).astype(jnp.int32)
            spot = jnp.where(pos >= MAIN, pos + 1, pos)
            slot = devs[p : p + 1] * BUCKET + (spot & 1) * HALF + (spot >> 1)
            slots_ref[p : p + 1, :] = jnp.where(keeps[p], slot, DUMMY)
            same = pos_iota == pos
            spreads.append(
                jnp.concatenate(
                    [
                        jnp.where(same, highs[p : p + 1], 0.0).astype(BF),
                        jnp.where(same, lows[p : p + 1], 0.0).astype(BF),
                    ],
                    axis=0,
                )
            )
        total = total + dot(hots[b], jnp.concatenate(spreads, axis=1), ((1,), (1,)))
        carry = carry + counts[b][:, BLOCK:]
    carry_ref[...] = carry
    place_ref[...] = total


def event_grads(step, event_ref, query_ref, up_ref, w1_ref, b1_ref, w2_ref, b2_ref, ws_ref, grad_ref):
    left_half = lax.broadcasted_iota(jnp.int32, (H1, 128), 1) < D
    row_at = lax.broadcasted_iota(jnp.int32, (16, 128), 0)
    lane_at = lax.broadcasted_iota(jnp.int32, (16, 128), 1)
    folds, ups, pre1, dscore, b2, ws, w2t_all, w2_all = ([] for _ in range(8))
    for k in range(STEP):
        f = step * STEP + k
        w1 = w1_ref[k]
        wa, wb, wc, wd = (w1[:, i * D : (i + 1) * D] for i in range(4))
        wad = wa + wd
        wbd = wb - wd
        wad = jnp.concatenate([wad, wad], axis=1)
        wcc = jnp.concatenate([wc, wc], axis=1)
        wbd = jnp.concatenate([wbd, jnp.zeros((H1, D), F32)], axis=1)
        b1_diag = diagonal(
            jnp.concatenate([b1_ref[pl.ds(f, 1), :], jnp.zeros((1, 128 - H1), F32)], axis=1), H1
        )
        b2.append(jnp.sum(diagonal(b2_ref[pl.ds(f, 1), :], H2_PAD), axis=1, keepdims=True))
        ws.append(jnp.sum(diagonal(ws_ref[pl.ds(f, 1), :], H2_PAD), axis=1, keepdims=True))
        w2t = jnp.concatenate([w2_ref[k], jnp.zeros((H2_PAD - H2, H1), F32)], axis=0)
        w2t_hi, w2t_lo = split(w2t)
        w2_hi, w2_lo = split(w2t.T)
        w2t_all.append(jnp.concatenate([w2t_hi, w2t_lo, w2t_hi], axis=1))
        w2_all.append(jnp.concatenate([w2_hi, w2_lo, w2_hi], axis=1))
        firsts = []
        for n in range(B_DEV):
            events = event_ref[n, k]
            query = query_ref[k, n : n + 1, :].astype(F32)
            up = up_ref[k, n : n + 1, :].astype(F32)
            query = jnp.concatenate([query, query], axis=1)
            up = jnp.concatenate([up, up], axis=1)
            folded = wad + wcc * query
            fold_hi = folded.astype(BF)
            fold_rest = folded - fold_hi.astype(F32)
            offset = jnp.sum(wbd * query + b1_diag, axis=1, keepdims=True)
            both = jnp.where(left_half, fold_hi.astype(F32), fold_rest).astype(BF)
            up_row = jnp.where((row_at == 0) & (lane_at < D), up, 0.0).astype(BF)
            first = dot(
                jnp.concatenate([both, up_row], axis=0), jnp.concatenate([events, events], axis=0)
            )
            firsts.append((first[:H1] + offset, first[H1 : H1 + 1]))
            folds.append((fold_hi, fold_rest.astype(BF)))
            ups.append(jnp.where(row_at < 2, up, 0.0).astype(BF))
        pre1.append(jnp.concatenate([first[0] for first in firsts], axis=1))
        dscore.append(jnp.concatenate([first[1] for first in firsts], axis=1))
    pre2, slope1, score, d1 = [], [], [], []
    for k in range(STEP):
        sig1 = 0.5 + 0.5 * jnp.tanh(0.5 * pre1[k])
        h1 = pre1[k] * sig1
        slope1.append(sig1 + h1 * (1.0 - sig1))
        h1_hi, h1_lo = split(h1)
        pre2.append(dot(w2t_all[k], jnp.concatenate([h1_hi, h1_hi, h1_lo], axis=0)) + b2[k])
    for k in range(STEP):
        sig2 = 0.5 + 0.5 * jnp.tanh(0.5 * pre2[k])
        h2 = pre2[k] * sig2
        slope2 = sig2 + h2 * (1.0 - sig2)
        score.append(jnp.sum(h2 * ws[k], axis=0, keepdims=True))
        d2_hi, d2_lo = split((dscore[k] * ws[k]) * slope2)
        d1.append(dot(w2_all[k], jnp.concatenate([d2_hi, d2_hi, d2_lo], axis=0)))
    for k in range(STEP):
        d1_hi, d1_lo = split(d1[k] * slope1[k])
        score_hi = score[k].astype(BF).astype(F32)
        score_lo = score[k] - score_hi
        for n in range(B_DEV):
            at = slice(n * LMAX, (n + 1) * LMAX)
            score_rows = jnp.where(
                row_at == 0, score_hi[:, at], jnp.where(row_at == 1, score_lo[:, at], 0.0)
            ).astype(BF)
            fold_hi, fold_lo = folds[k * B_DEV + n]
            row = (k * B_DEV + n) * LMAX
            grad_ref[row : row + LMAX, :] = dot(
                jnp.concatenate([d1_hi[:, at], d1_lo[:, at], d1_hi[:, at], score_rows], axis=0),
                jnp.concatenate([fold_hi, fold_hi, fold_lo, ups[k * B_DEV + n]], axis=0),
                ((0,), (0,)),
            )


def send_kernel(
    len_ref,
    cap_ref,
    table_ref,
    row_ref,
    places_ref,
    event_ref,
    query_ref,
    up_ref,
    w1_ref,
    b1_ref,
    w2_ref,
    b2_ref,
    ws_ref,
    main_ref,
    late_ref,
    earlier_ref,
    carry_ref,
    place_ref,
    slots_ref,
    index_ref,
    bucket_ref,
    grad_ref,
    pack_ref,
    rest_ref,
    slot_sem,
    sems,
):
    step = pl.program_id(0)

    def slot_copy():
        return pltpu.make_async_copy(slots_ref, index_ref, slot_sem)

    def scatter():
        for t in range(EVENTS):
            slot = index_ref[t // LMAX, t % LMAX]
            bucket_ref[pl.ds(slot, 1), :] = grad_ref[t : t + 1, :]

    @pl.when(step == 0)
    def _():
        rows = lax.broadcasted_iota(jnp.int32, (BLOCK, BLOCK + LMAX), 0)
        cols = lax.broadcasted_iota(jnp.int32, (BLOCK, BLOCK + LMAX), 1)
        earlier_ref[...] = jnp.where(rows < cols, 1.0, 0.0).astype(BF)
        carry_ref[...] = jnp.zeros_like(carry_ref)
        place_ref[...] = jnp.zeros_like(place_ref)
        slots_ref[...] = jnp.full(slots_ref.shape, DUMMY, jnp.int32)
        slot_copy().start()
        slot_copy().wait()

    scatter()
    rank_events(
        step, len_ref, cap_ref, table_ref, row_ref, places_ref, earlier_ref, carry_ref, place_ref,
        slots_ref,
    )
    event_grads(step, event_ref, query_ref, up_ref, w1_ref, b1_ref, w2_ref, b2_ref, ws_ref, grad_ref)
    slot_copy().start()
    slot_copy().wait()

    @pl.when(step == STEPS - 1)
    def _():
        scatter()
        parts = place_ref[...]
        high = pltpu.roll(parts, BUCKET, 1)
        lane = lax.broadcasted_iota(jnp.int32, parts.shape, 1)
        over = (jnp.max(carry_ref[...]) > float(MAIN)).astype(F32)
        spots = jnp.where(high > 0.0, high * 128.0 + parts - 128.0, float(ROWS_OWN))
        place_ref[...] = jnp.where(lane == 127, over, spots)
        main = pack_ref.reshape(DEVS * ROWS, 128)
        rest = rest_ref.reshape(DEVS * LATE, 128)
        lanes = lax.broadcasted_iota(jnp.int32, (HALF, 128), 1) < D

        def copies(chunk):
            part = pl.ds(chunk * CHUNK, CHUNK)
            return (
                pltpu.make_async_copy(pack_ref.at[part], main_ref.at[part], sems.at[0, chunk]),
                pltpu.make_async_copy(rest_ref.at[part], late_ref.at[part], sems.at[1, chunk]),
            )

        def pack(chunk, _):
            def two(k, _):
                pair = chunk * (CHUNK // 2) + k
                blocks = []
                for side in range(2):
                    dev = pair * 2 + side
                    at = pl.multiple_of(dev * BUCKET, BUCKET)
                    bucket_ref[pl.ds(at + HALF + ROWS - 1, 1), :] = place_ref[pl.ds(dev, 1), :]
                    left = bucket_ref[pl.ds(at, HALF), :]
                    right = bucket_ref[pl.ds(pl.multiple_of(at + HALF, HALF), HALF), :]
                    blocks.append(jnp.where(lanes, left, right))
                at = pl.multiple_of(pair * (2 * ROWS), 2 * ROWS)
                main[pl.ds(at, 2 * ROWS), :] = jnp.concatenate([b[:ROWS] for b in blocks], axis=0)
                at = pl.multiple_of(pair * (2 * LATE), 2 * LATE)
                rest[pl.ds(at, 2 * LATE), :] = jnp.concatenate([b[ROWS:] for b in blocks], axis=0)
                return 0

            lax.fori_loop(0, CHUNK // 2, two, 0, unroll=4)
            for copy in copies(chunk):
                copy.start()
            return 0

        def finish(chunk, _):
            for copy in copies(chunk):
                copy.wait()
            return 0

        lax.fori_loop(0, DEVS // CHUNK, pack, 0)
        lax.fori_loop(0, DEVS // CHUNK, finish, 0)


def add_kernel(in_ref, out_ref, over_ref, late_ref, new_ref, tail_ref, spot_ref, land_ref, turn_ref, sems, *sums):
    def rows_copy(k):
        part = pl.ds(k * PIECE, PIECE)
        return pltpu.make_async_copy(in_ref.at[part], new_ref.at[part], sems.at[1 + k])

    def spots_copy(k):
        part = pl.ds(k * PIECE, PIECE)
        return pltpu.make_async_copy(spot_ref.at[part], land_ref.at[part], sems.at[1 + PIECES + k])

    def table_copy(table):
        done = sems.at[1 + 2 * PIECES + table]
        return pltpu.make_async_copy(turn_ref.at[table], out_ref.at[table], done)

    tails = pltpu.make_async_copy(in_ref.at[:, ROWS - 1], tail_ref, sems.at[0])
    tails.start()
    for k in range(PIECES):
        rows_copy(k).start()

    def clear(i, _):
        at = pl.multiple_of(i * 64, 64)
        for total in sums:
            total[pl.ds(at, 64), :] = jnp.zeros((64, 128), F32)
        return 0

    lax.fori_loop(0, ROWS_OWN // 64, clear, 0)
    tails.wait()
    values = tail_ref.reshape(DEVS, 128)[...].astype(jnp.int32)
    lane = lax.broadcasted_iota(jnp.int32, values.shape, 1)
    over_ref[0, 0] = jnp.max(jnp.where(lane == 127, values, 0))
    late_ref[...] = values
    values = jnp.where((lane >= D) & (lane < D + MAIN), values, ROWS_OWN)
    filled = values < ROWS_OWN
    count = jnp.sum(filled.astype(jnp.int32), axis=1, keepdims=True)
    clash = jnp.zeros(values.shape, jnp.int32)
    for shift in range(2, 16, 2):
        moved = pltpu.roll(values, shift, 1)
        same = filled & (moved == values) & ((lane & 15) >= shift)
        clash = clash | same.astype(jnp.int32)
    clashes = jnp.sum(clash, axis=1, keepdims=True)
    later = pltpu.roll(jnp.where(clash > 0, values, ROWS_OWN), D, 1)
    spots = jnp.where(lane < D, later, jnp.where(clash > 0, ROWS_OWN, values))
    mode = jnp.where(count > 32, 1, 0) + jnp.where(clashes > 0, 2, 0)
    spot_ref[...] = jnp.where(lane == 60, mode, jnp.where(lane == 61, count, spots))
    for k in range(PIECES):
        spots_copy(k).start()

    def batch(s, start, stop):
        parts = []
        for first in range(start, stop, 8):
            rows = range(first, min(first + 8, stop))
            for side in range(2):
                total = sums[2 * (first // 8 % 2) + side]
                at = [land_ref[s, D + 2 * row + side] for row in rows]
                add = [
                    total[pl.ds(spot, 1), :] + new_ref[s, row] for spot, row in zip(at, rows)
                ]
                parts.append((total, at, add))
        for total, at, add in parts:
            for spot, value in zip(at, add):
                total[pl.ds(spot, 1), :] = value

    def sources(i, _):
        for k in range(ADD_STEP):
            batch(i * ADD_STEP + k, 0, 16)
        for k in range(ADD_STEP):
            s = i * ADD_STEP + k
            mode = land_ref[s, 60]

            @pl.when(mode > 0)
            def _():
                @pl.when((mode & 1) == 1)
                def _():
                    batch(s, 16, ROWS)

                @pl.when(mode >= 2)
                def _():
                    def single(j, _):
                        for side in range(2):
                            sums[side][pl.ds(land_ref[s, 2 * j + side], 1), :] += new_ref[s, j]
                        return 0

                    lax.fori_loop(0, (land_ref[s, 61] + 1) >> 1, single, 0)

        return 0

    def piece(k, _):
        spots_copy(k).wait()
        rows_copy(k).wait()
        lax.fori_loop(k * (PIECE // ADD_STEP), (k + 1) * (PIECE // ADD_STEP), sources, 0)
        return 0

    lax.fori_loop(0, PIECES, piece, 0)
    lanes = lax.broadcasted_iota(jnp.int32, (128, 128), 1) < D
    for table in range(TAB_OWN):
        for block in range(ROWS_DEV // 128):
            at = table * ROWS_DEV + block * 128
            at = slice(at, at + 128)
            joined = jnp.where(
                lanes, sums[0][at, :] + sums[2][at, :], sums[1][at, :] + sums[3][at, :]
            )
            turned = joined.T
            turn_ref[table, :, block * 128 : (block + 1) * 128] = turned[:D] + turned[D:]
        table_copy(table).start()
    for table in range(TAB_OWN):
        table_copy(table).wait()


def late_kernel(spot_ref, rest_ref, in_ref, out_ref):
    out_ref[...] = in_ref[...]
    lane = lax.broadcasted_iota(jnp.int32, (D, 128), 1)

    def source(s, _):
        for j in range(PLACES - MAIN):
            spot = spot_ref[s, j]

            @pl.when(spot < ROWS_OWN)
            def _():
                row = rest_ref[s, j // 2][:, (j % 2) * D : (j % 2 + 1) * D]
                column = jnp.sum(diagonal(row, D), axis=1, keepdims=True)
                at = pl.multiple_of((spot & 1023) >> 7 << 7, 128)
                added = jnp.where(lane == (spot & 127), column, 0.0)
                out_ref[spot >> 10, :, pl.ds(at, 128)] += added

        return 0

    lax.fori_loop(0, DEVS, source, 0)


def params(semantics=None):
    return pltpu.CompilerParams(vmem_limit_bytes=VMEM_BYTES, dimension_semantics=semantics)


def send_side(
    event_embed, target, pooled_grad, event_table, event_row, table_slot, lengths, caps,
    w_first, b_first, w_second, b_second, w_score,
):
    smem = pl.BlockSpec(memory_space=pltpu.SMEM)
    whole = lambda *shape: pl.BlockSpec(shape, lambda i: (0,) * len(shape))
    return pl.pallas_call(
        send_kernel,
        grid=(STEPS,),
        in_specs=[
            smem,
            smem,
            pl.BlockSpec((SPAN, LMAX), lambda i: (i, 0)),
            pl.BlockSpec((SPAN, LMAX), lambda i: (i, 0)),
            whole(1, LMAX),
            pl.BlockSpec((B_DEV, STEP, D, LMAX), lambda i: (0, i, 0, 0)),
            pl.BlockSpec((STEP, B_DEV, D), lambda i: (i, 0, 0)),
            pl.BlockSpec((STEP, B_DEV, D), lambda i: (i, 0, 0)),
            pl.BlockSpec((STEP, H1, 4 * D), lambda i: (i, 0, 0)),
            whole(F, H1),
            pl.BlockSpec((STEP, H2, H1), lambda i: (i, 0, 0)),
            whole(F, H2),
            whole(F, H2),
        ],
        out_specs=[pl.BlockSpec(memory_space=pl.ANY)] * 2,
        out_shape=[
            jax.ShapeDtypeStruct((DEVS, ROWS, 1, 128), F32),
            jax.ShapeDtypeStruct((DEVS, LATE, 1, 128), F32),
        ],
        scratch_shapes=[
            pltpu.VMEM((BLOCK, BLOCK + LMAX), BF),
            pltpu.VMEM((DEVS, LMAX), F32),
            pltpu.VMEM((DEVS, LMAX), F32),
            pltpu.VMEM((SPAN, LMAX), jnp.int32),
            pltpu.SMEM((SPAN, LMAX), jnp.int32),
            pltpu.VMEM((DUMMY + 8, 128), F32),
            pltpu.VMEM((EVENTS, 128), F32),
            pltpu.VMEM((DEVS, ROWS, 1, 128), F32),
            pltpu.VMEM((DEVS, LATE, 1, 128), F32),
            pltpu.SemaphoreType.DMA,
            pltpu.SemaphoreType.DMA((2, DEVS // CHUNK)),
        ],
        compiler_params=params(("arbitrary",)),
    )(
        lengths,
        caps,
        event_table.transpose(1, 0, 2).reshape(PAIRS, LMAX),
        event_row.transpose(1, 0, 2).reshape(PAIRS, LMAX),
        table_slot.reshape(1, -1),
        event_embed.transpose(0, 1, 3, 2),
        target.transpose(1, 0, 2),
        pooled_grad.transpose(1, 0, 2),
        w_first.transpose(0, 2, 1),
        b_first,
        w_second.transpose(0, 2, 1),
        b_second,
        w_score,
    )


def receive_side(arrived, late, exchange):
    summed, over, places = pl.pallas_call(
        add_kernel,
        in_specs=[pl.BlockSpec(memory_space=pl.ANY)],
        out_specs=[
            pl.BlockSpec(memory_space=pl.ANY),
            pl.BlockSpec(memory_space=pltpu.SMEM),
            pl.BlockSpec(memory_space=pltpu.VMEM),
        ],
        out_shape=[
            jax.ShapeDtypeStruct((TAB_OWN, D, ROWS_DEV), F32),
            jax.ShapeDtypeStruct((1, 1), jnp.int32),
            jax.ShapeDtypeStruct((DEVS, 128), jnp.int32),
        ],
        scratch_shapes=[
            pltpu.VMEM((DEVS, ROWS, 1, 128), F32),
            pltpu.VMEM((DEVS, 1, 128), F32),
            pltpu.VMEM((DEVS, 128), jnp.int32),
            pltpu.SMEM((DEVS, 128), jnp.int32),
            pltpu.VMEM((TAB_OWN, D, ROWS_DEV), F32),
            pltpu.SemaphoreType.DMA((1 + 2 * PIECES + TAB_OWN,)),
        ]
        + [pltpu.VMEM((ROWS_OWN + 8, 128), F32)] * 4,
        compiler_params=params(),
    )(arrived)

    def add_late(state):
        over, total = state
        spots = places[:, D + MAIN : D + PLACES]
        total = pl.pallas_call(
            late_kernel,
            in_specs=[pl.BlockSpec(memory_space=pltpu.SMEM)]
            + [pl.BlockSpec(memory_space=pltpu.VMEM)] * 2,
            out_specs=pl.BlockSpec(memory_space=pltpu.VMEM),
            out_shape=jax.ShapeDtypeStruct(total.shape, F32),
            compiler_params=params(),
        )(spots, exchange(late), total)
        return jnp.zeros_like(over), total

    _, summed = lax.while_loop(lambda state: state[0][0, 0] > 0, add_late, (over, summed))
    return summed.transpose(0, 2, 1)


def per_device(*args):
    main, late = send_side(*args)
    exchange = functools.partial(
        lax.all_to_all, axis_name=("group", "local"), split_axis=0, concat_axis=0, tiled=True
    )
    return receive_side(exchange(main), late, exchange)


def solution(mesh):
    parted = ("group", "local")
    in_specs = (
        P(parted, None, None, None),
        P(parted, None, None),
        P(parted, None, None),
        P(parted, None, None),
        P(parted, None, None),
        P(),
        P(parted, None),
        P(),
        P(),
        P(),
        P(),
        P(),
        P(),
    )
    return jax.shard_map(
        per_device, mesh=mesh, in_specs=in_specs, out_specs=P("group", "local", None), check_vma=False
    )
```

```python
import functools

import jax
import jax.numpy as jnp
from jax import lax
from jax.experimental import pallas as pl
from jax.experimental.pallas import tpu as pltpu
from jax.sharding import PartitionSpec as P

D = 64
F = 20
H1 = 80
H2 = 40
H2_PAD = 48
LMAX = 128
B_DEV = 4
TAB_OWN = 8
ROWS_DEV = 1024
GROUPS = 16
DEVS = 256
PAIRS = B_DEV * F
ROWS_OWN = TAB_OWN * ROWS_DEV
STEP = 2
STEPS = F // STEP
SPAN = STEP * B_DEV
EVENTS = SPAN * LMAX
BLOCK = 2 * LMAX
BUCKET = 64
HALF = 32
ROWS = 28
MAIN = 2 * ROWS - 1
LATE = HALF - ROWS
PLACES = 60
DUMMY = DEVS * BUCKET
CHUNK = 32
PIECES = 4
PIECE = DEVS // PIECES
ADD_STEP = 4
BF = jnp.bfloat16
F32 = jnp.float32
VMEM_BYTES = 63 * 1024 * 1024


def dot(left, right, contract=((1,), (0,))):
    return lax.dot_general(left, right, (contract, ((), ())), preferred_element_type=F32)


def diagonal(row, size):
    rows = lax.broadcasted_iota(jnp.int32, (size, row.shape[1]), 0)
    cols = lax.broadcasted_iota(jnp.int32, (size, row.shape[1]), 1)
    return jnp.where(rows == cols, row, 0.0)


def split(value):
    high = value.astype(BF)
    low = (value - high.astype(F32)).astype(BF)
    return high, low


def rank_events(step, len_ref, cap_ref, table_ref, row_ref, places_ref, earlier_ref, carry_ref, place_ref, slots_ref):
    block = pl.ds(pl.multiple_of(step * SPAN, SPAN), SPAN)
    table = table_ref[block, :]
    place = jnp.take_along_axis(
        jnp.broadcast_to(places_ref[...], table.shape), table, axis=1, mode="promise_in_bounds"
    )
    row = row_ref[block, :]
    devs = (row >> 10) * GROUPS + (place >> 3)
    owns = (place & 7) * ROWS_DEV + (row & 1023)
    highs = ((owns >> 7) + 1).astype(F32)
    lows = (owns & 127).astype(F32)
    lane = lax.broadcasted_iota(jnp.int32, (1, LMAX), 1)
    dev_iota = lax.broadcasted_iota(jnp.int32, (DEVS, LMAX), 0)
    pos_iota = lax.broadcasted_iota(jnp.int32, (BUCKET, LMAX), 0)
    keeps, hits, hots, counts = [], [], [], []
    for p in range(SPAN):
        f = step * STEP + p // B_DEV
        kept = lane < jnp.minimum(len_ref[p % B_DEV, f], cap_ref[f])
        keeps.append(kept)
        hits.append(dev_iota == jnp.where(kept, devs[p : p + 1], -1))
    for p in range(0, SPAN, 2):
        hot = jnp.concatenate(
            [jnp.where(hits[p + k], 1.0, 0.0).astype(BF) for k in range(2)], axis=1
        )
        hots.append(hot)
        counts.append(dot(hot, earlier_ref[...]))
    carry = carry_ref[...]
    total = place_ref[...]
    for b in range(SPAN // 2):
        spreads = []
        for k in range(2):
            p = 2 * b + k
            before = counts[b][:, k * LMAX : (k + 1) * LMAX] + carry
            pos = jnp.sum(jnp.where(hits[p], before, 0.0), axis=0, keepdims=True).astype(jnp.int32)
            spot = jnp.where(pos >= MAIN, pos + 1, pos)
            slot = devs[p : p + 1] * BUCKET + (spot & 1) * HALF + (spot >> 1)
            slots_ref[p : p + 1, :] = jnp.where(keeps[p], slot, DUMMY)
            same = pos_iota == pos
            spreads.append(
                jnp.concatenate(
                    [
                        jnp.where(same, highs[p : p + 1], 0.0).astype(BF),
                        jnp.where(same, lows[p : p + 1], 0.0).astype(BF),
                    ],
                    axis=0,
                )
            )
        total = total + dot(hots[b], jnp.concatenate(spreads, axis=1), ((1,), (1,)))
        carry = carry + counts[b][:, BLOCK:]
    carry_ref[...] = carry
    place_ref[...] = total


def event_grads(step, event_ref, query_ref, up_ref, w1_ref, b1_ref, w2_ref, b2_ref, ws_ref, grad_ref):
    left_half = lax.broadcasted_iota(jnp.int32, (H1, 128), 1) < D
    row_at = lax.broadcasted_iota(jnp.int32, (16, 128), 0)
    lane_at = lax.broadcasted_iota(jnp.int32, (16, 128), 1)
    folds, ups, pre1, dscore, b2, ws, w2t_all, w2_all = ([] for _ in range(8))
    for k in range(STEP):
        f = step * STEP + k
        w1 = w1_ref[f]
        wa, wb, wc, wd = (w1[:, i * D : (i + 1) * D] for i in range(4))
        wad = wa + wd
        wbd = wb - wd
        wad = jnp.concatenate([wad, wad], axis=1)
        wcc = jnp.concatenate([wc, wc], axis=1)
        wbd = jnp.concatenate([wbd, jnp.zeros((H1, D), F32)], axis=1)
        b1_diag = diagonal(
            jnp.concatenate([b1_ref[pl.ds(f, 1), :], jnp.zeros((1, 128 - H1), F32)], axis=1), H1
        )
        b2.append(jnp.sum(diagonal(b2_ref[pl.ds(f, 1), :], H2_PAD), axis=1, keepdims=True))
        ws.append(jnp.sum(diagonal(ws_ref[pl.ds(f, 1), :], H2_PAD), axis=1, keepdims=True))
        w2t = jnp.concatenate([w2_ref[f], jnp.zeros((H2_PAD - H2, H1), F32)], axis=0)
        w2t_hi, w2t_lo = split(w2t)
        w2_hi, w2_lo = split(w2t.T)
        w2t_all.append(jnp.concatenate([w2t_hi, w2t_lo, w2t_hi], axis=1))
        w2_all.append(jnp.concatenate([w2_hi, w2_lo, w2_hi], axis=1))
        firsts = []
        for n in range(B_DEV):
            events = event_ref[n, f]
            query = query_ref[f, n : n + 1, :].astype(F32)
            up = up_ref[f, n : n + 1, :].astype(F32)
            query = jnp.concatenate([query, query], axis=1)
            up = jnp.concatenate([up, up], axis=1)
            folded = wad + wcc * query
            fold_hi = folded.astype(BF)
            fold_rest = folded - fold_hi.astype(F32)
            offset = jnp.sum(wbd * query + b1_diag, axis=1, keepdims=True)
            both = jnp.where(left_half, fold_hi.astype(F32), fold_rest).astype(BF)
            up_row = jnp.where((row_at == 0) & (lane_at < D), up, 0.0).astype(BF)
            first = dot(
                jnp.concatenate([both, up_row], axis=0), jnp.concatenate([events, events], axis=0)
            )
            firsts.append((first[:H1] + offset, first[H1 : H1 + 1]))
            folds.append((fold_hi, fold_rest.astype(BF)))
            ups.append(jnp.where(row_at < 2, up, 0.0).astype(BF))
        pre1.append(jnp.concatenate([first[0] for first in firsts], axis=1))
        dscore.append(jnp.concatenate([first[1] for first in firsts], axis=1))
    pre2, slope1, score, d1 = [], [], [], []
    for k in range(STEP):
        sig1 = 0.5 + 0.5 * jnp.tanh(0.5 * pre1[k])
        h1 = pre1[k] * sig1
        slope1.append(sig1 + h1 * (1.0 - sig1))
        h1_hi, h1_lo = split(h1)
        pre2.append(dot(w2t_all[k], jnp.concatenate([h1_hi, h1_hi, h1_lo], axis=0)) + b2[k])
    for k in range(STEP):
        sig2 = 0.5 + 0.5 * jnp.tanh(0.5 * pre2[k])
        h2 = pre2[k] * sig2
        slope2 = sig2 + h2 * (1.0 - sig2)
        score.append(jnp.sum(h2 * ws[k], axis=0, keepdims=True))
        d2_hi, d2_lo = split((dscore[k] * ws[k]) * slope2)
        d1.append(dot(w2_all[k], jnp.concatenate([d2_hi, d2_hi, d2_lo], axis=0)))
    for k in range(STEP):
        d1_hi, d1_lo = split(d1[k] * slope1[k])
        score_hi = score[k].astype(BF).astype(F32)
        score_lo = score[k] - score_hi
        for n in range(B_DEV):
            at = slice(n * LMAX, (n + 1) * LMAX)
            score_rows = jnp.where(
                row_at == 0, score_hi[:, at], jnp.where(row_at == 1, score_lo[:, at], 0.0)
            ).astype(BF)
            fold_hi, fold_lo = folds[k * B_DEV + n]
            row = (k * B_DEV + n) * LMAX
            grad_ref[row : row + LMAX, :] = dot(
                jnp.concatenate([d1_hi[:, at], d1_lo[:, at], d1_hi[:, at], score_rows], axis=0),
                jnp.concatenate([fold_hi, fold_hi, fold_lo, ups[k * B_DEV + n]], axis=0),
                ((0,), (0,)),
            )


def send_kernel(
    len_ref,
    cap_ref,
    table_ref,
    row_ref,
    places_ref,
    event_ref,
    query_ref,
    up_ref,
    w1_ref,
    b1_ref,
    w2_ref,
    b2_ref,
    ws_ref,
    main_ref,
    late_ref,
    earlier_ref,
    carry_ref,
    place_ref,
    slots_ref,
    index_a_ref,
    index_b_ref,
    bucket_ref,
    grad_a_ref,
    grad_b_ref,
    pack_ref,
    rest_ref,
    slot_sems,
    sems,
):
    index_refs = (index_a_ref, index_b_ref)
    grad_refs = (grad_a_ref, grad_b_ref)

    def slot_copy(side):
        return pltpu.make_async_copy(slots_ref.at[side], index_refs[side], slot_sems.at[side])

    def scatter(side):
        for t in range(EVENTS):
            slot = index_refs[side][t // LMAX, t % LMAX]
            bucket_ref[pl.ds(slot, 1), :] = grad_refs[side][t : t + 1, :]

    rows = lax.broadcasted_iota(jnp.int32, (BLOCK, BLOCK + LMAX), 0)
    cols = lax.broadcasted_iota(jnp.int32, (BLOCK, BLOCK + LMAX), 1)
    earlier_ref[...] = jnp.where(rows < cols, 1.0, 0.0).astype(BF)
    carry_ref[...] = jnp.zeros_like(carry_ref)
    place_ref[...] = jnp.zeros_like(place_ref)
    slots_ref[...] = jnp.full(slots_ref.shape, DUMMY, jnp.int32)
    slot_copy(0).start()
    slot_copy(1).start()
    slot_copy(0).wait()

    def two_steps(i, _):
        for side in range(2):
            step = i * 2 + side
            scatter(side)
            rank_events(
                step, len_ref, cap_ref, table_ref, row_ref, places_ref, earlier_ref, carry_ref,
                place_ref, slots_ref.at[side],
            )
            event_grads(
                step, event_ref, query_ref, up_ref, w1_ref, b1_ref, w2_ref, b2_ref, ws_ref,
                grad_refs[side],
            )
            slot_copy(1 - side).wait()
            slot_copy(side).start()
        return 0

    lax.fori_loop(0, STEPS // 2, two_steps, 0)
    scatter(0)
    slot_copy(1).wait()
    scatter(1)
    parts = place_ref[...]
    high = pltpu.roll(parts, BUCKET, 1)
    lane = lax.broadcasted_iota(jnp.int32, parts.shape, 1)
    over = (jnp.max(carry_ref[...]) > float(MAIN)).astype(F32)
    spots = jnp.where(high > 0.0, high * 128.0 + parts - 128.0, float(ROWS_OWN))
    place_ref[...] = jnp.where(lane == 127, over, spots)
    lanes = lax.broadcasted_iota(jnp.int32, (HALF, 128), 1) < D

    def copies(chunk):
        part = pl.ds(chunk * (CHUNK * ROWS), CHUNK * ROWS)
        late = pl.ds(chunk * (CHUNK * LATE), CHUNK * LATE)
        return (
            pltpu.make_async_copy(pack_ref.at[part], main_ref.at[part], sems.at[0, chunk]),
            pltpu.make_async_copy(rest_ref.at[late], late_ref.at[late], sems.at[1, chunk]),
        )

    def pack(chunk, _):
        def two(k, _):
            pair = chunk * (CHUNK // 2) + k
            blocks = []
            for side in range(2):
                dev = pair * 2 + side
                at = pl.multiple_of(dev * BUCKET, BUCKET)
                bucket_ref[pl.ds(at + HALF + ROWS - 1, 1), :] = place_ref[pl.ds(dev, 1), :]
                left = bucket_ref[pl.ds(at, HALF), :]
                right = bucket_ref[pl.ds(pl.multiple_of(at + HALF, HALF), HALF), :]
                blocks.append(jnp.where(lanes, left, right))
            at = pl.multiple_of(pair * (2 * ROWS), 2 * ROWS)
            pack_ref[pl.ds(at, 2 * ROWS), :] = jnp.concatenate([b[:ROWS] for b in blocks], axis=0)
            at = pl.multiple_of(pair * (2 * LATE), 2 * LATE)
            rest_ref[pl.ds(at, 2 * LATE), :] = jnp.concatenate([b[ROWS:] for b in blocks], axis=0)
            return 0

        lax.fori_loop(0, CHUNK // 2, two, 0, unroll=4)
        for copy in copies(chunk):
            copy.start()
        return 0

    def finish(chunk, _):
        for copy in copies(chunk):
            copy.wait()
        return 0

    lax.fori_loop(0, DEVS // CHUNK, pack, 0)
    lax.fori_loop(0, DEVS // CHUNK, finish, 0)


def add_kernel(in_ref, out_ref, over_ref, late_ref, new_ref, tail_ref, spot_ref, land_ref, turn_ref, sems, *sums):
    def rows_copy(k):
        part = pl.ds(k * PIECE, PIECE)
        return pltpu.make_async_copy(in_ref.at[part], new_ref.at[part], sems.at[1 + k])

    def spots_copy(k):
        part = pl.ds(k * PIECE, PIECE)
        return pltpu.make_async_copy(spot_ref.at[part], land_ref.at[part], sems.at[1 + PIECES + k])

    def table_copy(table):
        done = sems.at[1 + 2 * PIECES + table]
        return pltpu.make_async_copy(turn_ref.at[table], out_ref.at[table], done)

    tails = pltpu.make_async_copy(in_ref.at[:, ROWS - 1], tail_ref, sems.at[0])
    tails.start()
    for k in range(PIECES):
        rows_copy(k).start()

    def clear(totals):
        def rows(i, _):
            at = pl.multiple_of(i * 64, 64)
            for total in totals:
                total[pl.ds(at, 64), :] = jnp.zeros((64, 128), F32)
            return 0

        lax.fori_loop(0, ROWS_OWN // 64, rows, 0)

    clear(sums[:2])
    tails.wait()
    values = tail_ref.reshape(DEVS, 128)[...].astype(jnp.int32)
    lane = lax.broadcasted_iota(jnp.int32, values.shape, 1)
    over_ref[0, 0] = jnp.max(jnp.where(lane == 127, values, 0))
    late_ref[...] = values
    values = jnp.where((lane >= D) & (lane < D + MAIN), values, ROWS_OWN)
    filled = values < ROWS_OWN
    count = jnp.sum(filled.astype(jnp.int32), axis=1, keepdims=True)
    clash = jnp.zeros(values.shape, jnp.int32)
    for shift in range(2, 16, 2):
        moved = pltpu.roll(values, shift, 1)
        same = filled & (moved == values) & ((lane & 15) >= shift)
        clash = clash | same.astype(jnp.int32)
    clashes = jnp.sum(clash, axis=1, keepdims=True)
    later = pltpu.roll(jnp.where(clash > 0, values, ROWS_OWN), D, 1)
    spots = jnp.where(lane < D, later, jnp.where(clash > 0, ROWS_OWN, values))
    mode = jnp.where(count > 32, 1, 0) + jnp.where(count > 40, 1, 0)
    mode = mode + jnp.where(clashes > 0, 4, 0)
    spot_ref[...] = jnp.where(lane == 60, mode, jnp.where(lane == 61, count, spots))
    for k in range(PIECES):
        spots_copy(k).start()
    clear(sums[2:])

    def batch(s, start, stop):
        parts = []
        for first in [start] + [row for row in range(start + 1, stop) if row % 8 == 0]:
            rows = range(first, min(first // 8 * 8 + 8, stop))
            for side in range(2):
                total = sums[2 * (first // 8 % 2) + side]
                at = [land_ref[s, D + 2 * row + side] for row in rows]
                add = [
                    total[pl.ds(spot, 1), :] + new_ref[s, row] for spot, row in zip(at, rows)
                ]
                parts.append((total, at, add))
        for total, at, add in parts:
            for spot, value in zip(at, add):
                total[pl.ds(spot, 1), :] = value

    def sources(i, _):
        for k in range(ADD_STEP):
            batch(i * ADD_STEP + k, 0, 16)
        for k in range(ADD_STEP):
            s = i * ADD_STEP + k
            mode = land_ref[s, 60]

            @pl.when(mode > 0)
            def _():
                @pl.when((mode & 3) > 0)
                def _():
                    batch(s, 16, 20)

                @pl.when((mode & 3) > 1)
                def _():
                    batch(s, 20, ROWS)

                @pl.when(mode >= 4)
                def _():
                    def single(j, _):
                        for side in range(2):
                            sums[side][pl.ds(land_ref[s, 2 * j + side], 1), :] += new_ref[s, j]
                        return 0

                    lax.fori_loop(0, (land_ref[s, 61] + 1) >> 1, single, 0)

        return 0

    def piece(k, _):
        spots_copy(k).wait()
        rows_copy(k).wait()
        lax.fori_loop(k * (PIECE // ADD_STEP), (k + 1) * (PIECE // ADD_STEP), sources, 0)
        return 0

    lax.fori_loop(0, PIECES, piece, 0)
    lanes = lax.broadcasted_iota(jnp.int32, (128, 128), 1) < D
    for table in range(TAB_OWN):
        for block in range(ROWS_DEV // 128):
            at = table * ROWS_DEV + block * 128
            at = slice(at, at + 128)
            joined = jnp.where(
                lanes, sums[0][at, :] + sums[2][at, :], sums[1][at, :] + sums[3][at, :]
            )
            turned = joined.T
            turn_ref[table, :, block * 128 : (block + 1) * 128] = turned[:D] + turned[D:]
        table_copy(table).start()
    for table in range(TAB_OWN):
        table_copy(table).wait()


def late_kernel(spot_ref, rest_ref, in_ref, out_ref):
    out_ref[...] = in_ref[...]
    lane = lax.broadcasted_iota(jnp.int32, (D, 128), 1)

    def source(s, _):
        for j in range(PLACES - MAIN):
            spot = spot_ref[s, j]

            @pl.when(spot < ROWS_OWN)
            def _():
                row = rest_ref[s, j // 2][:, (j % 2) * D : (j % 2 + 1) * D]
                column = jnp.sum(diagonal(row, D), axis=1, keepdims=True)
                at = pl.multiple_of((spot & 1023) >> 7 << 7, 128)
                added = jnp.where(lane == (spot & 127), column, 0.0)
                out_ref[spot >> 10, :, pl.ds(at, 128)] += added

        return 0

    lax.fori_loop(0, DEVS, source, 0)


def params():
    return pltpu.CompilerParams(vmem_limit_bytes=VMEM_BYTES)


def send_side(
    event_embed, target, pooled_grad, event_table, event_row, table_slot, lengths, caps,
    w_first, b_first, w_second, b_second, w_score,
):
    smem = pl.BlockSpec(memory_space=pltpu.SMEM)
    vmem = pl.BlockSpec(memory_space=pltpu.VMEM)
    return pl.pallas_call(
        send_kernel,
        in_specs=[smem] * 2 + [vmem] * 11,
        out_specs=[pl.BlockSpec(memory_space=pl.ANY)] * 2,
        out_shape=[
            jax.ShapeDtypeStruct((DEVS * ROWS, 128), F32),
            jax.ShapeDtypeStruct((DEVS * LATE, 128), F32),
        ],
        scratch_shapes=[
            pltpu.VMEM((BLOCK, BLOCK + LMAX), BF),
            pltpu.VMEM((DEVS, LMAX), F32),
            pltpu.VMEM((DEVS, LMAX), F32),
            pltpu.VMEM((2, SPAN, LMAX), jnp.int32),
            pltpu.SMEM((SPAN, LMAX), jnp.int32),
            pltpu.SMEM((SPAN, LMAX), jnp.int32),
            pltpu.VMEM((DUMMY + 8, 128), F32),
            pltpu.VMEM((EVENTS, 128), F32),
            pltpu.VMEM((EVENTS, 128), F32),
            pltpu.VMEM((DEVS * ROWS, 128), F32),
            pltpu.VMEM((DEVS * LATE, 128), F32),
            pltpu.SemaphoreType.DMA((2,)),
            pltpu.SemaphoreType.DMA((2, DEVS // CHUNK)),
        ],
        compiler_params=params(),
    )(
        lengths,
        caps,
        event_table.transpose(1, 0, 2).reshape(PAIRS, LMAX),
        event_row.transpose(1, 0, 2).reshape(PAIRS, LMAX),
        table_slot.reshape(1, -1),
        event_embed.transpose(0, 1, 3, 2),
        target.transpose(1, 0, 2),
        pooled_grad.transpose(1, 0, 2),
        w_first.transpose(0, 2, 1),
        b_first,
        w_second.transpose(0, 2, 1),
        b_second,
        w_score,
    )


def receive_side(arrived, late, exchange):
    summed, over, places = pl.pallas_call(
        add_kernel,
        in_specs=[pl.BlockSpec(memory_space=pl.ANY)],
        out_specs=[
            pl.BlockSpec(memory_space=pl.ANY),
            pl.BlockSpec(memory_space=pltpu.SMEM),
            pl.BlockSpec(memory_space=pltpu.VMEM),
        ],
        out_shape=[
            jax.ShapeDtypeStruct((TAB_OWN, D, ROWS_DEV), F32),
            jax.ShapeDtypeStruct((1, 1), jnp.int32),
            jax.ShapeDtypeStruct((DEVS, 128), jnp.int32),
        ],
        scratch_shapes=[
            pltpu.VMEM((DEVS, ROWS, 1, 128), F32),
            pltpu.VMEM((DEVS, 1, 128), F32),
            pltpu.VMEM((DEVS, 128), jnp.int32),
            pltpu.SMEM((DEVS, 128), jnp.int32),
            pltpu.VMEM((TAB_OWN, D, ROWS_DEV), F32),
            pltpu.SemaphoreType.DMA((1 + 2 * PIECES + TAB_OWN,)),
        ]
        + [pltpu.VMEM((ROWS_OWN + 8, 128), F32)] * 4,
        compiler_params=params(),
    )(arrived)

    def add_late(state):
        over, total = state
        spots = places[:, D + MAIN : D + PLACES]
        total = pl.pallas_call(
            late_kernel,
            in_specs=[pl.BlockSpec(memory_space=pltpu.SMEM)]
            + [pl.BlockSpec(memory_space=pltpu.VMEM)] * 2,
            out_specs=pl.BlockSpec(memory_space=pltpu.VMEM),
            out_shape=jax.ShapeDtypeStruct(total.shape, F32),
            compiler_params=params(),
        )(spots, exchange(late), total)
        return jnp.zeros_like(over), total

    _, summed = lax.while_loop(lambda state: state[0][0, 0] > 0, add_late, (over, summed))
    return summed.transpose(0, 2, 1)


def per_device(*args):
    main, late = send_side(*args)
    main = main.reshape(DEVS, ROWS, 1, 128)
    late = late.reshape(DEVS, LATE, 1, 128)
    exchange = functools.partial(
        lax.all_to_all, axis_name=("local", "group"), split_axis=0, concat_axis=0, tiled=True
    )
    return receive_side(exchange(main), late, exchange)


def solution(mesh):
    parted = ("group", "local")
    in_specs = (
        P(parted, None, None, None),
        P(parted, None, None),
        P(parted, None, None),
        P(parted, None, None),
        P(parted, None, None),
        P(),
        P(parted, None),
        P(),
        P(),
        P(),
        P(),
        P(),
        P(),
    )
    return jax.shard_map(
        per_device, mesh=mesh, in_specs=in_specs, out_specs=P("group", "local", None), check_vma=False
    )
```

```python
import functools

import jax
import jax.numpy as jnp
from jax import lax
from jax.experimental import pallas as pl
from jax.experimental.pallas import tpu as pltpu
from jax.sharding import PartitionSpec as P

D = 64
F = 20
H1 = 80
H2 = 40
H2_PAD = 48
LMAX = 128
B_DEV = 4
TAB_OWN = 8
ROWS_DEV = 1024
GROUPS = 16
DEVS = 256
PAIRS = B_DEV * F
ROWS_OWN = TAB_OWN * ROWS_DEV
STEP = 2
STEPS = F // STEP
SPAN = STEP * B_DEV
EVENTS = SPAN * LMAX
BLOCK = 2 * LMAX
BUCKET = 64
HALF = 32
ROWS = 28
MAIN = 2 * ROWS - 1
LATE = HALF - ROWS
PLACES = 60
DUMMY = DEVS * BUCKET
CHUNK = 32
PIECES = 8
PIECE = DEVS // PIECES
ADD_STEP = 4
BF = jnp.bfloat16
F32 = jnp.float32
VMEM_BYTES = 63 * 1024 * 1024


def dot(left, right, contract=((1,), (0,))):
    return lax.dot_general(left, right, (contract, ((), ())), preferred_element_type=F32)


def diagonal(row, size):
    rows = lax.broadcasted_iota(jnp.int32, (size, row.shape[1]), 0)
    cols = lax.broadcasted_iota(jnp.int32, (size, row.shape[1]), 1)
    return jnp.where(rows == cols, row, 0.0)


def split(value):
    high = value.astype(BF)
    low = (value - high.astype(F32)).astype(BF)
    return high, low


def rank_events(step, len_ref, cap_ref, table_ref, row_ref, places_ref, earlier_ref, carry_ref, place_ref, slots_ref):
    block = pl.ds(pl.multiple_of(step * SPAN, SPAN), SPAN)
    table = table_ref[block, :]
    place = jnp.take_along_axis(
        jnp.broadcast_to(places_ref[...], table.shape), table, axis=1, mode="promise_in_bounds"
    )
    row = row_ref[block, :]
    devs = (row >> 10) * GROUPS + (place >> 3)
    owns = (place & 7) * ROWS_DEV + (row & 1023)
    highs = ((owns >> 7) + 1).astype(F32)
    lows = (owns & 127).astype(F32)
    lane = lax.broadcasted_iota(jnp.int32, (1, LMAX), 1)
    dev_iota = lax.broadcasted_iota(jnp.int32, (DEVS, LMAX), 0)
    pos_iota = lax.broadcasted_iota(jnp.int32, (BUCKET, LMAX), 0)
    keeps, hits, hots, counts = [], [], [], []
    for p in range(SPAN):
        f = step * STEP + p // B_DEV
        kept = lane < jnp.minimum(len_ref[p % B_DEV, f], cap_ref[f])
        keeps.append(kept)
        hits.append(dev_iota == jnp.where(kept, devs[p : p + 1], -1))
    for p in range(0, SPAN, 2):
        hot = jnp.concatenate(
            [jnp.where(hits[p + k], 1.0, 0.0).astype(BF) for k in range(2)], axis=1
        )
        hots.append(hot)
        counts.append(dot(hot, earlier_ref[...]))
    carry = carry_ref[...]
    total = place_ref[...]
    for b in range(SPAN // 2):
        spreads = []
        for k in range(2):
            p = 2 * b + k
            before = counts[b][:, k * LMAX : (k + 1) * LMAX] + carry
            pos = jnp.sum(jnp.where(hits[p], before, 0.0), axis=0, keepdims=True).astype(jnp.int32)
            spot = jnp.where(pos >= MAIN, pos + 1, pos)
            slot = devs[p : p + 1] * BUCKET + (spot & 1) * HALF + (spot >> 1)
            slots_ref[p : p + 1, :] = jnp.where(keeps[p], slot, DUMMY)
            same = pos_iota == pos
            spreads.append(
                jnp.concatenate(
                    [
                        jnp.where(same, highs[p : p + 1], 0.0).astype(BF),
                        jnp.where(same, lows[p : p + 1], 0.0).astype(BF),
                    ],
                    axis=0,
                )
            )
        total = total + dot(hots[b], jnp.concatenate(spreads, axis=1), ((1,), (1,)))
        carry = carry + counts[b][:, BLOCK:]
    carry_ref[...] = carry
    place_ref[...] = total


def event_grads(step, event_ref, query_ref, up_ref, w1_ref, b1_ref, w2_ref, b2_ref, ws_ref, grad_ref):
    left_half = lax.broadcasted_iota(jnp.int32, (H1, 128), 1) < D
    row_at = lax.broadcasted_iota(jnp.int32, (16, 128), 0)
    lane_at = lax.broadcasted_iota(jnp.int32, (16, 128), 1)
    folds, ups, pre1, dscore, b2, ws, w2t_all, w2_all = ([] for _ in range(8))
    for k in range(STEP):
        f = step * STEP + k
        w1 = w1_ref[f]
        wa, wb, wc, wd = (w1[:, i * D : (i + 1) * D] for i in range(4))
        wad = wa + wd
        wbd = wb - wd
        wad = jnp.concatenate([wad, wad], axis=1)
        wcc = jnp.concatenate([wc, wc], axis=1)
        wbd = jnp.concatenate([wbd, jnp.zeros((H1, D), F32)], axis=1)
        b1_diag = diagonal(
            jnp.concatenate([b1_ref[pl.ds(f, 1), :], jnp.zeros((1, 128 - H1), F32)], axis=1), H1
        )
        b2.append(jnp.sum(diagonal(b2_ref[pl.ds(f, 1), :], H2_PAD), axis=1, keepdims=True))
        ws.append(jnp.sum(diagonal(ws_ref[pl.ds(f, 1), :], H2_PAD), axis=1, keepdims=True))
        w2t = jnp.concatenate([w2_ref[f], jnp.zeros((H2_PAD - H2, H1), F32)], axis=0)
        w2t_hi, w2t_lo = split(w2t)
        w2_hi, w2_lo = split(w2t.T)
        w2t_all.append(jnp.concatenate([w2t_hi, w2t_lo, w2t_hi], axis=1))
        w2_all.append(jnp.concatenate([w2_hi, w2_lo, w2_hi], axis=1))
        firsts = []
        for n in range(B_DEV):
            events = event_ref[n, f]
            query = query_ref[f, n : n + 1, :].astype(F32)
            up = up_ref[f, n : n + 1, :].astype(F32)
            query = jnp.concatenate([query, query], axis=1)
            up = jnp.concatenate([up, up], axis=1)
            folded = wad + wcc * query
            fold_hi = folded.astype(BF)
            fold_rest = folded - fold_hi.astype(F32)
            offset = jnp.sum(wbd * query + b1_diag, axis=1, keepdims=True)
            both = jnp.where(left_half, fold_hi.astype(F32), fold_rest).astype(BF)
            up_row = jnp.where((row_at == 0) & (lane_at < D), up, 0.0).astype(BF)
            first = dot(
                jnp.concatenate([both, up_row], axis=0), jnp.concatenate([events, events], axis=0)
            )
            firsts.append((first[:H1] + offset, first[H1 : H1 + 1]))
            folds.append((fold_hi, fold_rest.astype(BF)))
            ups.append(jnp.where(row_at < 2, up, 0.0).astype(BF))
        pre1.append(jnp.concatenate([first[0] for first in firsts], axis=1))
        dscore.append(jnp.concatenate([first[1] for first in firsts], axis=1))
    pre2, slope1, score, d1 = [], [], [], []
    for k in range(STEP):
        sig1 = 0.5 + 0.5 * jnp.tanh(0.5 * pre1[k])
        h1 = pre1[k] * sig1
        slope1.append(sig1 + h1 * (1.0 - sig1))
        h1_hi, h1_lo = split(h1)
        pre2.append(dot(w2t_all[k], jnp.concatenate([h1_hi, h1_hi, h1_lo], axis=0)) + b2[k])
    for k in range(STEP):
        sig2 = 0.5 + 0.5 * jnp.tanh(0.5 * pre2[k])
        h2 = pre2[k] * sig2
        slope2 = sig2 + h2 * (1.0 - sig2)
        score.append(jnp.sum(h2 * ws[k], axis=0, keepdims=True))
        d2_hi, d2_lo = split((dscore[k] * ws[k]) * slope2)
        d1.append(dot(w2_all[k], jnp.concatenate([d2_hi, d2_hi, d2_lo], axis=0)))
    for k in range(STEP):
        d1_hi, d1_lo = split(d1[k] * slope1[k])
        score_hi = score[k].astype(BF).astype(F32)
        score_lo = score[k] - score_hi
        for n in range(B_DEV):
            at = slice(n * LMAX, (n + 1) * LMAX)
            score_rows = jnp.where(
                row_at == 0, score_hi[:, at], jnp.where(row_at == 1, score_lo[:, at], 0.0)
            ).astype(BF)
            fold_hi, fold_lo = folds[k * B_DEV + n]
            row = (k * B_DEV + n) * LMAX
            parts = dot(
                d1_hi[:, at], jnp.concatenate([fold_hi, fold_lo], axis=1), ((0,), (0,))
            )
            rest = dot(
                jnp.concatenate([d1_lo[:, at], score_rows], axis=0),
                jnp.concatenate([fold_hi, ups[k * B_DEV + n]], axis=0),
                ((0,), (0,)),
            )
            grad_ref[row : row + LMAX, :] = parts[:, :128] + parts[:, 128:] + rest


def send_kernel(
    len_ref,
    cap_ref,
    table_ref,
    row_ref,
    places_ref,
    event_ref,
    query_ref,
    up_ref,
    w1_ref,
    b1_ref,
    w2_ref,
    b2_ref,
    ws_ref,
    main_ref,
    late_ref,
    earlier_ref,
    carry_ref,
    place_ref,
    slots_ref,
    index_a_ref,
    index_b_ref,
    bucket_ref,
    grad_a_ref,
    grad_b_ref,
    pack_ref,
    rest_ref,
    slot_sems,
    sems,
):
    index_refs = (index_a_ref, index_b_ref)
    grad_refs = (grad_a_ref, grad_b_ref)

    def slot_copy(side):
        return pltpu.make_async_copy(slots_ref.at[side], index_refs[side], slot_sems.at[side])

    def scatter(side):
        for t in range(EVENTS):
            slot = index_refs[side][t // LMAX, t % LMAX]
            bucket_ref[pl.ds(slot, 1), :] = grad_refs[side][t : t + 1, :]

    rows = lax.broadcasted_iota(jnp.int32, (BLOCK, BLOCK + LMAX), 0)
    cols = lax.broadcasted_iota(jnp.int32, (BLOCK, BLOCK + LMAX), 1)
    earlier_ref[...] = jnp.where(rows < cols, 1.0, 0.0).astype(BF)
    carry_ref[...] = jnp.zeros_like(carry_ref)
    place_ref[...] = jnp.zeros_like(place_ref)
    slots_ref[...] = jnp.full(slots_ref.shape, DUMMY, jnp.int32)
    slot_copy(0).start()
    slot_copy(1).start()
    slot_copy(0).wait()

    def two_steps(i, _):
        for side in range(2):
            step = i * 2 + side
            scatter(side)
            rank_events(
                step, len_ref, cap_ref, table_ref, row_ref, places_ref, earlier_ref, carry_ref,
                place_ref, slots_ref.at[side],
            )
            event_grads(
                step, event_ref, query_ref, up_ref, w1_ref, b1_ref, w2_ref, b2_ref, ws_ref,
                grad_refs[side],
            )
            slot_copy(1 - side).wait()
            slot_copy(side).start()
        return 0

    lax.fori_loop(0, STEPS // 2, two_steps, 0)
    scatter(0)
    slot_copy(1).wait()
    scatter(1)
    parts = place_ref[...]
    high = pltpu.roll(parts, BUCKET, 1)
    lane = lax.broadcasted_iota(jnp.int32, parts.shape, 1)
    over = (jnp.max(carry_ref[...]) > float(MAIN)).astype(F32)
    spots = jnp.where(high > 0.0, high * 128.0 + parts - 128.0, float(ROWS_OWN))
    place_ref[...] = jnp.where(lane == 127, over, spots)
    lanes = lax.broadcasted_iota(jnp.int32, (HALF, 128), 1) < D

    def copies(chunk):
        part = pl.ds(chunk * (CHUNK * ROWS), CHUNK * ROWS)
        late = pl.ds(chunk * (CHUNK * LATE), CHUNK * LATE)
        return (
            pltpu.make_async_copy(pack_ref.at[part], main_ref.at[part], sems.at[0, chunk]),
            pltpu.make_async_copy(rest_ref.at[late], late_ref.at[late], sems.at[1, chunk]),
        )

    def pack(chunk, _):
        def two(k, _):
            pair = chunk * (CHUNK // 2) + k
            blocks = []
            for side in range(2):
                dev = pair * 2 + side
                at = pl.multiple_of(dev * BUCKET, BUCKET)
                bucket_ref[pl.ds(at + HALF + ROWS - 1, 1), :] = place_ref[pl.ds(dev, 1), :]
                left = bucket_ref[pl.ds(at, HALF), :]
                right = bucket_ref[pl.ds(pl.multiple_of(at + HALF, HALF), HALF), :]
                blocks.append(jnp.where(lanes, left, right))
            at = pl.multiple_of(pair * (2 * ROWS), 2 * ROWS)
            pack_ref[pl.ds(at, 2 * ROWS), :] = jnp.concatenate([b[:ROWS] for b in blocks], axis=0)
            at = pl.multiple_of(pair * (2 * LATE), 2 * LATE)
            rest_ref[pl.ds(at, 2 * LATE), :] = jnp.concatenate([b[ROWS:] for b in blocks], axis=0)
            return 0

        lax.fori_loop(0, CHUNK // 2, two, 0, unroll=4)
        for copy in copies(chunk):
            copy.start()
        return 0

    def finish(chunk, _):
        for copy in copies(chunk):
            copy.wait()
        return 0

    lax.fori_loop(0, DEVS // CHUNK, pack, 0)
    lax.fori_loop(0, DEVS // CHUNK, finish, 0)


def add_kernel(in_ref, out_ref, over_ref, late_ref, new_ref, tail_ref, spot_ref, land_ref, turn_ref, sems, *sums):
    def rows_copy(k):
        part = pl.ds(k * PIECE, PIECE)
        return pltpu.make_async_copy(in_ref.at[part], new_ref.at[part], sems.at[1 + k])

    def spots_copy(k):
        part = pl.ds(k * PIECE, PIECE)
        return pltpu.make_async_copy(spot_ref.at[part], land_ref.at[part], sems.at[1 + PIECES + k])

    def table_copy(table):
        done = sems.at[1 + 2 * PIECES + table]
        return pltpu.make_async_copy(turn_ref.at[table], out_ref.at[table], done)

    tails = pltpu.make_async_copy(in_ref.at[:, ROWS - 1], tail_ref, sems.at[0])
    tails.start()
    for k in range(PIECES):
        rows_copy(k).start()

    def clear(totals):
        def rows(i, _):
            at = pl.multiple_of(i * 64, 64)
            for total in totals:
                total[pl.ds(at, 64), :] = jnp.zeros((64, 128), F32)
            return 0

        lax.fori_loop(0, ROWS_OWN // 64, rows, 0)

    clear(sums[:2])
    tails.wait()
    values = tail_ref.reshape(DEVS, 128)[...].astype(jnp.int32)
    lane = lax.broadcasted_iota(jnp.int32, values.shape, 1)
    over_ref[0, 0] = jnp.max(jnp.where(lane == 127, values, 0))
    late_ref[...] = values
    values = jnp.where((lane >= D) & (lane < D + MAIN), values, ROWS_OWN)
    filled = values < ROWS_OWN
    count = jnp.sum(filled.astype(jnp.int32), axis=1, keepdims=True)
    clash = jnp.zeros(values.shape, jnp.int32)
    for shift in range(2, 16, 2):
        moved = pltpu.roll(values, shift, 1)
        same = filled & (moved == values) & ((lane & 15) >= shift)
        clash = clash | same.astype(jnp.int32)
    clashes = jnp.sum(clash, axis=1, keepdims=True)
    later = pltpu.roll(jnp.where(clash > 0, values, ROWS_OWN), D, 1)
    spots = jnp.where(lane < D, later, jnp.where(clash > 0, ROWS_OWN, values))
    mode = jnp.where(count > 32, 1, 0) + jnp.where(count > 40, 1, 0)
    mode = mode + jnp.where(clashes > 0, 4, 0)
    spot_ref[...] = jnp.where(lane == 60, mode, jnp.where(lane == 61, count, spots))
    for k in range(PIECES):
        spots_copy(k).start()
    clear(sums[2:])

    def batch(s, start, stop):
        parts = []
        for first in [start] + [row for row in range(start + 1, stop) if row % 8 == 0]:
            rows = range(first, min(first // 8 * 8 + 8, stop))
            for side in range(2):
                total = sums[2 * (first // 8 % 2) + side]
                at = [land_ref[s, D + 2 * row + side] for row in rows]
                add = [
                    total[pl.ds(spot, 1), :] + new_ref[s, row] for spot, row in zip(at, rows)
                ]
                parts.append((total, at, add))
        for total, at, add in parts:
            for spot, value in zip(at, add):
                total[pl.ds(spot, 1), :] = value

    def sources(i, _):
        for k in range(ADD_STEP):
            batch(i * ADD_STEP + k, 0, 16)
        for k in range(ADD_STEP):
            s = i * ADD_STEP + k
            mode = land_ref[s, 60]

            @pl.when(mode > 0)
            def _():
                @pl.when((mode & 3) > 0)
                def _():
                    batch(s, 16, 20)

                @pl.when((mode & 3) > 1)
                def _():
                    batch(s, 20, ROWS)

                @pl.when(mode >= 4)
                def _():
                    def single(j, _):
                        for side in range(2):
                            sums[side][pl.ds(land_ref[s, 2 * j + side], 1), :] += new_ref[s, j]
                        return 0

                    lax.fori_loop(0, (land_ref[s, 61] + 1) >> 1, single, 0)

        return 0

    def piece(k, _):
        spots_copy(k).wait()
        rows_copy(k).wait()
        lax.fori_loop(k * (PIECE // ADD_STEP), (k + 1) * (PIECE // ADD_STEP), sources, 0)
        return 0

    lax.fori_loop(0, PIECES, piece, 0)
    lanes = lax.broadcasted_iota(jnp.int32, (128, 128), 1) < D
    for table in range(TAB_OWN):
        for block in range(ROWS_DEV // 128):
            at = table * ROWS_DEV + block * 128
            at = slice(at, at + 128)
            joined = jnp.where(
                lanes, sums[0][at, :] + sums[2][at, :], sums[1][at, :] + sums[3][at, :]
            )
            turned = joined.T
            turn_ref[table, :, block * 128 : (block + 1) * 128] = turned[:D] + turned[D:]
        table_copy(table).start()
    for table in range(TAB_OWN):
        table_copy(table).wait()


def late_kernel(spot_ref, rest_ref, in_ref, out_ref):
    out_ref[...] = in_ref[...]
    lane = lax.broadcasted_iota(jnp.int32, (D, 128), 1)

    def source(s, _):
        for j in range(PLACES - MAIN):
            spot = spot_ref[s, j]

            @pl.when(spot < ROWS_OWN)
            def _():
                row = rest_ref[s, j // 2][:, (j % 2) * D : (j % 2 + 1) * D]
                column = jnp.sum(diagonal(row, D), axis=1, keepdims=True)
                at = pl.multiple_of((spot & 1023) >> 7 << 7, 128)
                added = jnp.where(lane == (spot & 127), column, 0.0)
                out_ref[spot >> 10, :, pl.ds(at, 128)] += added

        return 0

    lax.fori_loop(0, DEVS, source, 0)


def params():
    return pltpu.CompilerParams(vmem_limit_bytes=VMEM_BYTES)


def send_side(
    event_embed, target, pooled_grad, event_table, event_row, table_slot, lengths, caps,
    w_first, b_first, w_second, b_second, w_score,
):
    smem = pl.BlockSpec(memory_space=pltpu.SMEM)
    vmem = pl.BlockSpec(memory_space=pltpu.VMEM)
    return pl.pallas_call(
        send_kernel,
        in_specs=[smem] * 2 + [vmem] * 11,
        out_specs=[pl.BlockSpec(memory_space=pl.ANY)] * 2,
        out_shape=[
            jax.ShapeDtypeStruct((DEVS * ROWS, 128), F32),
            jax.ShapeDtypeStruct((DEVS * LATE, 128), F32),
        ],
        scratch_shapes=[
            pltpu.VMEM((BLOCK, BLOCK + LMAX), BF),
            pltpu.VMEM((DEVS, LMAX), F32),
            pltpu.VMEM((DEVS, LMAX), F32),
            pltpu.VMEM((2, SPAN, LMAX), jnp.int32),
            pltpu.SMEM((SPAN, LMAX), jnp.int32),
            pltpu.SMEM((SPAN, LMAX), jnp.int32),
            pltpu.VMEM((DUMMY + 8, 128), F32),
            pltpu.VMEM((EVENTS, 128), F32),
            pltpu.VMEM((EVENTS, 128), F32),
            pltpu.VMEM((DEVS * ROWS, 128), F32),
            pltpu.VMEM((DEVS * LATE, 128), F32),
            pltpu.SemaphoreType.DMA((2,)),
            pltpu.SemaphoreType.DMA((2, DEVS // CHUNK)),
        ],
        compiler_params=params(),
    )(
        lengths,
        caps,
        event_table.transpose(1, 0, 2).reshape(PAIRS, LMAX),
        event_row.transpose(1, 0, 2).reshape(PAIRS, LMAX),
        table_slot.reshape(1, -1),
        event_embed.transpose(0, 1, 3, 2),
        target.transpose(1, 0, 2),
        pooled_grad.transpose(1, 0, 2),
        w_first.transpose(0, 2, 1),
        b_first,
        w_second.transpose(0, 2, 1),
        b_second,
        w_score,
    )


def receive_side(arrived, late, exchange):
    summed, over, places = pl.pallas_call(
        add_kernel,
        in_specs=[pl.BlockSpec(memory_space=pl.ANY)],
        out_specs=[
            pl.BlockSpec(memory_space=pl.ANY),
            pl.BlockSpec(memory_space=pltpu.SMEM),
            pl.BlockSpec(memory_space=pltpu.VMEM),
        ],
        out_shape=[
            jax.ShapeDtypeStruct((TAB_OWN, D, ROWS_DEV), F32),
            jax.ShapeDtypeStruct((1, 1), jnp.int32),
            jax.ShapeDtypeStruct((DEVS, 128), jnp.int32),
        ],
        scratch_shapes=[
            pltpu.VMEM((DEVS, ROWS, 1, 128), F32),
            pltpu.VMEM((DEVS, 1, 128), F32),
            pltpu.VMEM((DEVS, 128), jnp.int32),
            pltpu.SMEM((DEVS, 128), jnp.int32),
            pltpu.VMEM((TAB_OWN, D, ROWS_DEV), F32),
            pltpu.SemaphoreType.DMA((1 + 2 * PIECES + TAB_OWN,)),
        ]
        + [pltpu.VMEM((ROWS_OWN + 8, 128), F32)] * 4,
        compiler_params=params(),
    )(arrived)

    def add_late(state):
        over, total = state
        spots = places[:, D + MAIN : D + PLACES]
        total = pl.pallas_call(
            late_kernel,
            in_specs=[pl.BlockSpec(memory_space=pltpu.SMEM)]
            + [pl.BlockSpec(memory_space=pltpu.VMEM)] * 2,
            out_specs=pl.BlockSpec(memory_space=pltpu.VMEM),
            out_shape=jax.ShapeDtypeStruct(total.shape, F32),
            compiler_params=params(),
        )(spots, exchange(late), total)
        return jnp.zeros_like(over), total

    _, summed = lax.while_loop(lambda state: state[0][0, 0] > 0, add_late, (over, summed))
    return summed.transpose(0, 2, 1)


def per_device(*args):
    main, late = send_side(*args)
    main = main.reshape(DEVS, ROWS, 1, 128)
    late = late.reshape(DEVS, LATE, 1, 128)
    exchange = functools.partial(
        lax.all_to_all, axis_name=("local", "group"), split_axis=0, concat_axis=0, tiled=True
    )
    return receive_side(exchange(main), late, exchange)


def solution(mesh):
    parted = ("group", "local")
    in_specs = (
        P(parted, None, None, None),
        P(parted, None, None),
        P(parted, None, None),
        P(parted, None, None),
        P(parted, None, None),
        P(),
        P(parted, None),
        P(),
        P(),
        P(),
        P(),
        P(),
        P(),
    )
    return jax.shard_map(
        per_device, mesh=mesh, in_specs=in_specs, out_specs=P("group", "local", None), check_vma=False
    )
```

```python
import functools

import jax
import jax.numpy as jnp
from jax import lax
from jax.experimental import pallas as pl
from jax.experimental.pallas import tpu as pltpu
from jax.sharding import PartitionSpec as P

D = 64
F = 20
H1 = 80
H2 = 40
H2_PAD = 48
LMAX = 128
B_DEV = 4
TAB_OWN = 8
ROWS_DEV = 1024
GROUPS = 16
DEVS = 256
PAIRS = B_DEV * F
ROWS_OWN = TAB_OWN * ROWS_DEV
STEP = 2
STEPS = F // STEP
SPAN = STEP * B_DEV
EVENTS = SPAN * LMAX
BLOCK = 2 * LMAX
BUCKET = 64
HALF = 32
ROWS = 28
MAIN = 2 * ROWS - 1
LATE = HALF - ROWS
PLACES = 60
DUMMY = DEVS * BUCKET
CHUNK = 32
PIECES = 8
PIECE = DEVS // PIECES
ADD_STEP = 4
BF = jnp.bfloat16
F32 = jnp.float32
VMEM_BYTES = 63 * 1024 * 1024


def dot(left, right, contract=((1,), (0,))):
    return lax.dot_general(left, right, (contract, ((), ())), preferred_element_type=F32)


def diagonal(row, size):
    rows = lax.broadcasted_iota(jnp.int32, (size, row.shape[1]), 0)
    cols = lax.broadcasted_iota(jnp.int32, (size, row.shape[1]), 1)
    return jnp.where(rows == cols, row, 0.0)


def split(value):
    high = value.astype(BF)
    low = (value - high.astype(F32)).astype(BF)
    return high, low


def rank_events(step, len_ref, cap_ref, table_ref, row_ref, places_ref, earlier_ref, carry_ref, place_ref, slots_ref):
    block = pl.ds(pl.multiple_of(step * SPAN, SPAN), SPAN)
    table = table_ref[block, :]
    place = jnp.take_along_axis(
        jnp.broadcast_to(places_ref[...], table.shape), table, axis=1, mode="promise_in_bounds"
    )
    row = row_ref[block, :]
    devs = (row >> 10) * GROUPS + (place >> 3)
    owns = (place & 7) * ROWS_DEV + (row & 1023)
    highs = ((owns >> 7) + 1).astype(F32)
    lows = (owns & 127).astype(F32)
    lane = lax.broadcasted_iota(jnp.int32, (1, LMAX), 1)
    dev_iota = lax.broadcasted_iota(jnp.int32, (DEVS, LMAX), 0)
    pos_iota = lax.broadcasted_iota(jnp.int32, (BUCKET, LMAX), 0)
    keeps, hits, hots, counts = [], [], [], []
    for p in range(SPAN):
        f = step * STEP + p // B_DEV
        kept = lane < jnp.minimum(len_ref[p % B_DEV, f], cap_ref[f])
        keeps.append(kept)
        hits.append(dev_iota == jnp.where(kept, devs[p : p + 1], -1))
    for p in range(0, SPAN, 2):
        hot = jnp.concatenate(
            [jnp.where(hits[p + k], 1.0, 0.0).astype(BF) for k in range(2)], axis=1
        )
        hots.append(hot)
        counts.append(dot(hot, earlier_ref[...]))
    carry = carry_ref[...]
    total = place_ref[...]
    for b in range(SPAN // 2):
        spreads = []
        for k in range(2):
            p = 2 * b + k
            before = counts[b][:, k * LMAX : (k + 1) * LMAX] + carry
            pos = jnp.sum(jnp.where(hits[p], before, 0.0), axis=0, keepdims=True).astype(jnp.int32)
            spot = jnp.where(pos >= MAIN, pos + 1, pos)
            slot = devs[p : p + 1] * BUCKET + (spot & 1) * HALF + (spot >> 1)
            slots_ref[p : p + 1, :] = jnp.where(keeps[p], slot, DUMMY)
            same = pos_iota == pos
            spreads.append(
                jnp.concatenate(
                    [
                        jnp.where(same, highs[p : p + 1], 0.0).astype(BF),
                        jnp.where(same, lows[p : p + 1], 0.0).astype(BF),
                    ],
                    axis=0,
                )
            )
        total = total + dot(hots[b], jnp.concatenate(spreads, axis=1), ((1,), (1,)))
        carry = carry + counts[b][:, BLOCK:]
    carry_ref[...] = carry
    place_ref[...] = total


def event_grads(step, event_ref, query_ref, up_ref, w1_ref, b1_ref, w2_ref, b2_ref, ws_ref, grad_ref):
    left_half = lax.broadcasted_iota(jnp.int32, (H1, 128), 1) < D
    row_at = lax.broadcasted_iota(jnp.int32, (16, 128), 0)
    lane_at = lax.broadcasted_iota(jnp.int32, (16, 128), 1)
    folds, ups, pre1, dscore, b2, ws, w2t_all, w2_all = ([] for _ in range(8))
    w2s = jnp.concatenate(
        [
            jnp.concatenate([w2_ref[step * STEP + k], jnp.zeros((64 - H2, H1), F32)], axis=0)
            for k in range(STEP)
        ],
        axis=0,
    ).T
    for k in range(STEP):
        f = step * STEP + k
        w1 = w1_ref[f]
        wa, wb, wc, wd = (w1[:, i * D : (i + 1) * D] for i in range(4))
        wad = wa + wd
        wbd = wb - wd
        wad = jnp.concatenate([wad, wad], axis=1)
        wcc = jnp.concatenate([wc, wc], axis=1)
        wbd = jnp.concatenate([wbd, jnp.zeros((H1, D), F32)], axis=1)
        b1_diag = diagonal(
            jnp.concatenate([b1_ref[pl.ds(f, 1), :], jnp.zeros((1, 128 - H1), F32)], axis=1), H1
        )
        b2.append(jnp.sum(diagonal(b2_ref[pl.ds(f, 1), :], H2_PAD), axis=1, keepdims=True))
        ws.append(jnp.sum(diagonal(ws_ref[pl.ds(f, 1), :], H2_PAD), axis=1, keepdims=True))
        w2t = jnp.concatenate([w2_ref[f], jnp.zeros((H2_PAD - H2, H1), F32)], axis=0)
        w2t_hi, w2t_lo = split(w2t)
        w2_hi, w2_lo = split(w2s[:, k * 64 : k * 64 + H2_PAD])
        w2t_all.append(jnp.concatenate([w2t_hi, w2t_lo, w2t_hi], axis=1))
        w2_all.append(jnp.concatenate([w2_hi, w2_lo, w2_hi], axis=1))
        firsts = []
        for n in range(B_DEV):
            events = event_ref[n, f]
            query = query_ref[f, n : n + 1, :].astype(F32)
            up = up_ref[f, n : n + 1, :].astype(F32)
            query = jnp.concatenate([query, query], axis=1)
            up = jnp.concatenate([up, up], axis=1)
            folded = wad + wcc * query
            fold_hi = folded.astype(BF)
            fold_rest = folded - fold_hi.astype(F32)
            offset = jnp.sum(wbd * query + b1_diag, axis=1, keepdims=True)
            both = jnp.where(left_half, fold_hi.astype(F32), fold_rest).astype(BF)
            up_row = jnp.where((row_at == 0) & (lane_at < D), up, 0.0).astype(BF)
            first = dot(
                jnp.concatenate([both, up_row], axis=0), jnp.concatenate([events, events], axis=0)
            )
            firsts.append((first[:H1] + offset, first[H1 : H1 + 1]))
            folds.append((fold_hi, fold_rest.astype(BF)))
            ups.append(jnp.where(row_at < 2, up, 0.0).astype(BF))
        pre1.append(jnp.concatenate([first[0] for first in firsts], axis=1))
        dscore.append(jnp.concatenate([first[1] for first in firsts], axis=1))
    pre2, slope1, score, d1 = [], [], [], []
    for k in range(STEP):
        sig1 = 0.5 + 0.5 * jnp.tanh(0.5 * pre1[k])
        h1 = pre1[k] * sig1
        slope1.append(sig1 + h1 * (1.0 - sig1))
        h1_hi, h1_lo = split(h1)
        pre2.append(dot(w2t_all[k], jnp.concatenate([h1_hi, h1_hi, h1_lo], axis=0)) + b2[k])
    for k in range(STEP):
        sig2 = 0.5 + 0.5 * jnp.tanh(0.5 * pre2[k])
        h2 = pre2[k] * sig2
        slope2 = sig2 + h2 * (1.0 - sig2)
        score.append(jnp.sum(h2 * ws[k], axis=0, keepdims=True))
        d2_hi, d2_lo = split((dscore[k] * ws[k]) * slope2)
        d1.append(dot(w2_all[k], jnp.concatenate([d2_hi, d2_hi, d2_lo], axis=0)))
    for k in range(STEP):
        d1_hi, d1_lo = split(d1[k] * slope1[k])
        score_hi = score[k].astype(BF).astype(F32)
        score_lo = score[k] - score_hi
        for n in range(B_DEV):
            at = slice(n * LMAX, (n + 1) * LMAX)
            score_rows = jnp.where(
                row_at == 0, score_hi[:, at], jnp.where(row_at == 1, score_lo[:, at], 0.0)
            ).astype(BF)
            fold_hi, fold_lo = folds[k * B_DEV + n]
            row = (k * B_DEV + n) * LMAX
            parts = dot(
                d1_hi[:, at], jnp.concatenate([fold_hi, fold_lo], axis=1), ((0,), (0,))
            )
            rest = dot(
                jnp.concatenate([d1_lo[:, at], score_rows], axis=0),
                jnp.concatenate([fold_hi, ups[k * B_DEV + n]], axis=0),
                ((0,), (0,)),
            )
            grad_ref[row : row + LMAX, :] = parts[:, :128] + parts[:, 128:] + rest


def send_kernel(
    len_ref,
    cap_ref,
    table_ref,
    row_ref,
    places_ref,
    event_ref,
    query_ref,
    up_ref,
    w1_ref,
    b1_ref,
    w2_ref,
    b2_ref,
    ws_ref,
    main_ref,
    late_ref,
    earlier_ref,
    carry_ref,
    place_ref,
    slots_ref,
    index_a_ref,
    index_b_ref,
    bucket_ref,
    grad_a_ref,
    grad_b_ref,
    pack_ref,
    rest_ref,
    slot_sems,
    sems,
):
    index_refs = (index_a_ref, index_b_ref)
    grad_refs = (grad_a_ref, grad_b_ref)

    def slot_copy(side):
        return pltpu.make_async_copy(slots_ref.at[side], index_refs[side], slot_sems.at[side])

    def scatter(side):
        for t in range(EVENTS):
            slot = index_refs[side][t // LMAX, t % LMAX]
            bucket_ref[pl.ds(slot, 1), :] = grad_refs[side][t : t + 1, :]

    rows = lax.broadcasted_iota(jnp.int32, (BLOCK, BLOCK + LMAX), 0)
    cols = lax.broadcasted_iota(jnp.int32, (BLOCK, BLOCK + LMAX), 1)
    earlier_ref[...] = jnp.where(rows < cols, 1.0, 0.0).astype(BF)
    carry_ref[...] = jnp.zeros_like(carry_ref)
    place_ref[...] = jnp.zeros_like(place_ref)
    slots_ref[...] = jnp.full(slots_ref.shape, DUMMY, jnp.int32)
    slot_copy(0).start()
    slot_copy(1).start()
    slot_copy(0).wait()

    def two_steps(i, _):
        for side in range(2):
            step = i * 2 + side
            scatter(side)
            rank_events(
                step, len_ref, cap_ref, table_ref, row_ref, places_ref, earlier_ref, carry_ref,
                place_ref, slots_ref.at[side],
            )
            event_grads(
                step, event_ref, query_ref, up_ref, w1_ref, b1_ref, w2_ref, b2_ref, ws_ref,
                grad_refs[side],
            )
            slot_copy(1 - side).wait()
            slot_copy(side).start()
        return 0

    lax.fori_loop(0, STEPS // 2, two_steps, 0)
    scatter(0)
    slot_copy(1).wait()
    scatter(1)
    parts = place_ref[...]
    high = pltpu.roll(parts, BUCKET, 1)
    lane = lax.broadcasted_iota(jnp.int32, parts.shape, 1)
    over = (jnp.max(carry_ref[...]) > float(MAIN)).astype(F32)
    spots = jnp.where(high > 0.0, high * 128.0 + parts - 128.0, float(ROWS_OWN))
    place_ref[...] = jnp.where(lane == 127, over, spots)
    lanes = lax.broadcasted_iota(jnp.int32, (HALF, 128), 1) < D

    def copies(chunk):
        part = pl.ds(chunk * (CHUNK * ROWS), CHUNK * ROWS)
        late = pl.ds(chunk * (CHUNK * LATE), CHUNK * LATE)
        return (
            pltpu.make_async_copy(pack_ref.at[part], main_ref.at[part], sems.at[0, chunk]),
            pltpu.make_async_copy(rest_ref.at[late], late_ref.at[late], sems.at[1, chunk]),
        )

    def pack(chunk, _):
        def two(k, _):
            pair = chunk * (CHUNK // 2) + k
            blocks = []
            for side in range(2):
                dev = pair * 2 + side
                at = pl.multiple_of(dev * BUCKET, BUCKET)
                bucket_ref[pl.ds(at + HALF + ROWS - 1, 1), :] = place_ref[pl.ds(dev, 1), :]
                left = bucket_ref[pl.ds(at, HALF), :]
                right = bucket_ref[pl.ds(pl.multiple_of(at + HALF, HALF), HALF), :]
                blocks.append(jnp.where(lanes, left, right))
            at = pl.multiple_of(pair * (2 * ROWS), 2 * ROWS)
            pack_ref[pl.ds(at, 2 * ROWS), :] = jnp.concatenate([b[:ROWS] for b in blocks], axis=0)
            at = pl.multiple_of(pair * (2 * LATE), 2 * LATE)
            rest_ref[pl.ds(at, 2 * LATE), :] = jnp.concatenate([b[ROWS:] for b in blocks], axis=0)
            return 0

        lax.fori_loop(0, CHUNK // 2, two, 0, unroll=4)
        for copy in copies(chunk):
            copy.start()
        return 0

    def finish(chunk, _):
        for copy in copies(chunk):
            copy.wait()
        return 0

    lax.fori_loop(0, DEVS // CHUNK, pack, 0)
    lax.fori_loop(0, DEVS // CHUNK, finish, 0)


def add_kernel(in_ref, out_ref, over_ref, late_ref, new_ref, tail_ref, spot_ref, land_ref, turn_ref, sems, *sums):
    def rows_copy(k):
        part = pl.ds(k * PIECE, PIECE)
        return pltpu.make_async_copy(in_ref.at[part], new_ref.at[part], sems.at[1 + k])

    def spots_copy(k):
        part = pl.ds(k * PIECE, PIECE)
        return pltpu.make_async_copy(spot_ref.at[part], land_ref.at[part], sems.at[1 + PIECES + k])

    def table_copy(table):
        done = sems.at[1 + 2 * PIECES + table]
        return pltpu.make_async_copy(turn_ref.at[table], out_ref.at[table], done)

    tails = pltpu.make_async_copy(in_ref.at[:, ROWS - 1], tail_ref, sems.at[0])
    tails.start()
    for k in range(PIECES):
        rows_copy(k).start()

    def clear(totals):
        def rows(i, _):
            at = pl.multiple_of(i * 64, 64)
            for total in totals:
                total[pl.ds(at, 64), :] = jnp.zeros((64, 128), F32)
            return 0

        lax.fori_loop(0, ROWS_OWN // 64, rows, 0)

    clear(sums[:2])
    tails.wait()
    values = tail_ref.reshape(DEVS, 128)[...].astype(jnp.int32)
    lane = lax.broadcasted_iota(jnp.int32, values.shape, 1)
    over_ref[0, 0] = jnp.max(jnp.where(lane == 127, values, 0))
    late_ref[...] = values
    values = jnp.where((lane >= D) & (lane < D + MAIN), values, ROWS_OWN)
    filled = values < ROWS_OWN
    count = jnp.sum(filled.astype(jnp.int32), axis=1, keepdims=True)
    clash = jnp.zeros(values.shape, jnp.int32)
    for shift in range(2, 16, 2):
        moved = pltpu.roll(values, shift, 1)
        same = filled & (moved == values) & ((lane & 15) >= shift)
        clash = clash | same.astype(jnp.int32)
    clashes = jnp.sum(clash, axis=1, keepdims=True)
    later = pltpu.roll(jnp.where(clash > 0, values, ROWS_OWN), D, 1)
    spots = jnp.where(lane < D, later, jnp.where(clash > 0, ROWS_OWN, values))
    mode = jnp.where(count > 32, 1, 0) + jnp.where(count > 40, 1, 0)
    mode = mode + jnp.where(clashes > 0, 4, 0)
    spot_ref[...] = jnp.where(lane == 60, mode, jnp.where(lane == 61, count, spots))
    for k in range(PIECES):
        spots_copy(k).start()
    clear(sums[2:])

    def batch(s, start, stop):
        parts = []
        for first in [start] + [row for row in range(start + 1, stop) if row % 8 == 0]:
            rows = range(first, min(first // 8 * 8 + 8, stop))
            for side in range(2):
                total = sums[2 * (first // 8 % 2) + side]
                at = [land_ref[s, D + 2 * row + side] for row in rows]
                add = [
                    total[pl.ds(spot, 1), :] + new_ref[s, row] for spot, row in zip(at, rows)
                ]
                parts.append((total, at, add))
        for total, at, add in parts:
            for spot, value in zip(at, add):
                total[pl.ds(spot, 1), :] = value

    def sources(i, _):
        for k in range(ADD_STEP):
            batch(i * ADD_STEP + k, 0, 16)
        for k in range(ADD_STEP):
            s = i * ADD_STEP + k
            mode = land_ref[s, 60]

            @pl.when(mode > 0)
            def _():
                @pl.when((mode & 3) > 0)
                def _():
                    batch(s, 16, 20)

                @pl.when((mode & 3) > 1)
                def _():
                    batch(s, 20, ROWS)

                @pl.when(mode >= 4)
                def _():
                    def single(j, _):
                        for side in range(2):
                            sums[side][pl.ds(land_ref[s, 2 * j + side], 1), :] += new_ref[s, j]
                        return 0

                    lax.fori_loop(0, (land_ref[s, 61] + 1) >> 1, single, 0)

        return 0

    def piece(k, _):
        spots_copy(k).wait()
        rows_copy(k).wait()
        lax.fori_loop(k * (PIECE // ADD_STEP), (k + 1) * (PIECE // ADD_STEP), sources, 0)
        return 0

    lax.fori_loop(0, PIECES, piece, 0)
    lanes = lax.broadcasted_iota(jnp.int32, (128, 128), 1) < D
    for table in range(TAB_OWN):
        for block in range(ROWS_DEV // 128):
            at = table * ROWS_DEV + block * 128
            at = slice(at, at + 128)
            joined = jnp.where(
                lanes, sums[0][at, :] + sums[2][at, :], sums[1][at, :] + sums[3][at, :]
            )
            turned = joined.T
            turn_ref[table, :, block * 128 : (block + 1) * 128] = turned[:D] + turned[D:]
        table_copy(table).start()
    for table in range(TAB_OWN):
        table_copy(table).wait()


def late_kernel(spot_ref, rest_ref, in_ref, out_ref):
    out_ref[...] = in_ref[...]
    lane = lax.broadcasted_iota(jnp.int32, (D, 128), 1)

    def source(s, _):
        for j in range(PLACES - MAIN):
            spot = spot_ref[s, j]

            @pl.when(spot < ROWS_OWN)
            def _():
                row = rest_ref[s, j // 2][:, (j % 2) * D : (j % 2 + 1) * D]
                column = jnp.sum(diagonal(row, D), axis=1, keepdims=True)
                at = pl.multiple_of((spot & 1023) >> 7 << 7, 128)
                added = jnp.where(lane == (spot & 127), column, 0.0)
                out_ref[spot >> 10, :, pl.ds(at, 128)] += added

        return 0

    lax.fori_loop(0, DEVS, source, 0)


def params():
    return pltpu.CompilerParams(vmem_limit_bytes=VMEM_BYTES)


def send_side(
    event_embed, target, pooled_grad, event_table, event_row, table_slot, lengths, caps,
    w_first, b_first, w_second, b_second, w_score,
):
    smem = pl.BlockSpec(memory_space=pltpu.SMEM)
    vmem = pl.BlockSpec(memory_space=pltpu.VMEM)
    return pl.pallas_call(
        send_kernel,
        in_specs=[smem] * 2 + [vmem] * 11,
        out_specs=[pl.BlockSpec(memory_space=pl.ANY)] * 2,
        out_shape=[
            jax.ShapeDtypeStruct((DEVS * ROWS, 128), F32),
            jax.ShapeDtypeStruct((DEVS * LATE, 128), F32),
        ],
        scratch_shapes=[
            pltpu.VMEM((BLOCK, BLOCK + LMAX), BF),
            pltpu.VMEM((DEVS, LMAX), F32),
            pltpu.VMEM((DEVS, LMAX), F32),
            pltpu.VMEM((2, SPAN, LMAX), jnp.int32),
            pltpu.SMEM((SPAN, LMAX), jnp.int32),
            pltpu.SMEM((SPAN, LMAX), jnp.int32),
            pltpu.VMEM((DUMMY + 8, 128), F32),
            pltpu.VMEM((EVENTS, 128), F32),
            pltpu.VMEM((EVENTS, 128), F32),
            pltpu.VMEM((DEVS * ROWS, 128), F32),
            pltpu.VMEM((DEVS * LATE, 128), F32),
            pltpu.SemaphoreType.DMA((2,)),
            pltpu.SemaphoreType.DMA((2, DEVS // CHUNK)),
        ],
        compiler_params=params(),
    )(
        lengths,
        caps,
        event_table.transpose(1, 0, 2).reshape(PAIRS, LMAX),
        event_row.transpose(1, 0, 2).reshape(PAIRS, LMAX),
        table_slot.reshape(1, -1),
        event_embed.transpose(0, 1, 3, 2),
        target.transpose(1, 0, 2),
        pooled_grad.transpose(1, 0, 2),
        w_first.transpose(0, 2, 1),
        b_first,
        w_second.transpose(0, 2, 1),
        b_second,
        w_score,
    )


def receive_side(arrived, late, exchange):
    summed, over, places = pl.pallas_call(
        add_kernel,
        in_specs=[pl.BlockSpec(memory_space=pl.ANY)],
        out_specs=[
            pl.BlockSpec(memory_space=pl.ANY),
            pl.BlockSpec(memory_space=pltpu.SMEM),
            pl.BlockSpec(memory_space=pltpu.VMEM),
        ],
        out_shape=[
            jax.ShapeDtypeStruct((TAB_OWN, D, ROWS_DEV), F32),
            jax.ShapeDtypeStruct((1, 1), jnp.int32),
            jax.ShapeDtypeStruct((DEVS, 128), jnp.int32),
        ],
        scratch_shapes=[
            pltpu.VMEM((DEVS, ROWS, 1, 128), F32),
            pltpu.VMEM((DEVS, 1, 128), F32),
            pltpu.VMEM((DEVS, 128), jnp.int32),
            pltpu.SMEM((DEVS, 128), jnp.int32),
            pltpu.VMEM((TAB_OWN, D, ROWS_DEV), F32),
            pltpu.SemaphoreType.DMA((1 + 2 * PIECES + TAB_OWN,)),
        ]
        + [pltpu.VMEM((ROWS_OWN + 8, 128), F32)] * 4,
        compiler_params=params(),
    )(arrived)

    def add_late(state):
        over, total = state
        spots = places[:, D + MAIN : D + PLACES]
        total = pl.pallas_call(
            late_kernel,
            in_specs=[pl.BlockSpec(memory_space=pltpu.SMEM)]
            + [pl.BlockSpec(memory_space=pltpu.VMEM)] * 2,
            out_specs=pl.BlockSpec(memory_space=pltpu.VMEM),
            out_shape=jax.ShapeDtypeStruct(total.shape, F32),
            compiler_params=params(),
        )(spots, exchange(late), total)
        return jnp.zeros_like(over), total

    _, summed = lax.while_loop(lambda state: state[0][0, 0] > 0, add_late, (over, summed))
    return summed.transpose(0, 2, 1)


def per_device(*args):
    main, late = send_side(*args)
    main = main.reshape(DEVS, ROWS, 1, 128)
    late = late.reshape(DEVS, LATE, 1, 128)
    exchange = functools.partial(
        lax.all_to_all, axis_name=("local", "group"), split_axis=0, concat_axis=0, tiled=True
    )
    return receive_side(exchange(main), late, exchange)


def solution(mesh):
    parted = ("group", "local")
    in_specs = (
        P(parted, None, None, None),
        P(parted, None, None),
        P(parted, None, None),
        P(parted, None, None),
        P(parted, None, None),
        P(),
        P(parted, None),
        P(),
        P(),
        P(),
        P(),
        P(),
        P(),
    )
    return jax.shard_map(
        per_device, mesh=mesh, in_specs=in_specs, out_specs=P("group", "local", None), check_vma=False
    )
```
